1024 devices in a mesh: row: 64 (over y, z_lo), col: 16 (over x, z_hi, core).
Axes of the slice: x: 4, y: 8, z: 16 (z_hi: 2, z_lo: 8; z = z_hi * 8 + z_lo), core: 2. Of those that a mesh axis runs over, the one named last changes fastest.
Arguments:
- images: float32 [16384, 768], P(('row', 'col')), may hold values from -0.21650635 to 0.21650635
- texts: float32 [16384, 768], P(('row', 'col')), may hold values from -0.21650635 to 0.21650635
- log_temp: float32 [1], replicated, may hold values from 2 to 2.6
- bias: float32 [1], replicated, may hold values from -7 to -5
Outputs:
- loss: float32 [1], replicated
- d_log_temp: float32 [1], replicated
- d_bias: float32 [1], replicated
- grad_images: float32 [16384, 768], P(('row', 'col'))
- grad_texts: float32 [16384, 768], P(('row', 'col'))
The draws below stay inside these ranges and needn't reach their ends.
All inputs are finite; a program needn't handle non-finite values.
Results may differ from the reference program's by a relative error of at most 0.0003.
Values sent between devices are 32-bit elements; how exact they have to be, the bound alone decides.
No kernel may reach another device: no remote copies, remote signals or barrier semaphores. Data moves between devices by JAX's collectives and lax.ppermute only.
A program may use at most 32 MiB of HBM per device.

```python
import jax
import jax.numpy as jnp
from jax import lax

D = 768
BATCH = 16384


def shard_levels(stream_key, shape, pieces, smallest, top_value):
    factor_of, own = 1.0, jax.random.fold_in(stream_key, 6)
    for axis_at, parts in pieces:
        draws = jnp.exp(jax.random.uniform(jax.random.fold_in(own, axis_at), (parts,), jnp.float32, smallest / len(pieces), top_value / len(pieces)))
        factor_of = factor_of * jnp.repeat(draws, shape[axis_at] // parts).reshape([-1 if axis == axis_at else 1 for axis in range(len(shape))])
    return factor_of


def bell_draw(rng, dims, width, reach, cuts=(), kind=jnp.bfloat16):
    result = jax.random.normal(rng, dims, jnp.float32) * width
    if len(cuts) > 0:
        result = shard_levels(rng, dims, cuts, -0.22, 0.18) * result
    return jnp.clip(result, min=-reach, max=reach).astype(kind)


def setup_inputs(seed: int = 0) -> dict:
    key_of = jax.random.split(jax.random.key(seed), 5)
    images = bell_draw(key_of[0], (BATCH, D), (D ** -0.5), 0.21650635, ((0, 1024),), jnp.float32)
    texts = bell_draw(key_of[1], (BATCH, D), (D ** -0.5), 0.21650635, ((0, 1024),), jnp.float32)
    log_temp = jnp.clip(jax.random.uniform(key_of[2], (1,), jnp.float32, 2.0, 2.6), 2.0, 2.6)
    bias = jnp.clip(jax.random.uniform(key_of[3], (1,), jnp.float32, -7.0, -5.0), -7.0, -5.0)
    return {"images": images, "texts": texts, "log_temp": log_temp, "bias": bias}


def normalize(x):
    norm = jnp.sqrt(lax.optimization_barrier(jnp.sum(x * x, axis=1, keepdims=True)) + 1e-06)
    return x / norm

def reference(images, texts, log_temp, bias):
    unit_img, back_img = jax.vjp(normalize, images)
    unit_txt, back_txt = jax.vjp(normalize, texts)
    temp = jnp.exp(log_temp[0])
    shift = bias[0]
    total_rows = unit_img.shape[0]
    blk = min(total_rows, 1024)
    count = total_rows // blk
    columns = jnp.arange(total_rows, dtype=jnp.int32)

    def step(carry, index):
        grad_txt, loss_sum, temp_sum, bias_sum = carry
        start = (index * blk).astype(jnp.int32)
        block = lax.dynamic_slice_in_dim(unit_img, start, blk, 0)
        sim = jnp.dot(block, unit_txt.T, precision=lax.Precision.HIGHEST, preferred_element_type=jnp.float32)
        logit = temp * sim + shift
        rows = start + jnp.arange(blk, dtype=jnp.int32)
        sign = jnp.where(rows[:, None] == columns[None, :], 1.0, -1.0).astype(jnp.float32)
        pair_grad = -sign * jax.nn.sigmoid(-sign * logit)
        loss_sum = loss_sum + jnp.sum(jax.nn.softplus(-sign * logit))
        temp_sum = temp_sum + jnp.sum(pair_grad * sim)
        bias_sum = bias_sum + jnp.sum(pair_grad)
        grad_blk = temp * jnp.dot(pair_grad, unit_txt, precision=lax.Precision.HIGHEST, preferred_element_type=jnp.float32)
        grad_txt = grad_txt + temp * jnp.dot(pair_grad.T, block, precision=lax.Precision.HIGHEST, preferred_element_type=jnp.float32)
        return ((grad_txt, loss_sum, temp_sum, bias_sum), grad_blk)
    zero = jnp.zeros((), jnp.float32)
    init = (jnp.zeros(unit_txt.shape, jnp.float32), zero, zero, zero)
    (grad_txt, loss_sum, temp_sum, bias_sum), blocks = lax.scan(step, init, jnp.arange(count, dtype=jnp.int32))
    grad_img = blocks.reshape(unit_img.shape)
    grad_images = back_img(grad_img)[0]
    grad_texts = back_txt(grad_txt)[0]
    scale = jnp.float32(total_rows)
    loss = jnp.reshape(loss_sum / scale, (1,))
    d_log_temp = jnp.reshape(temp * temp_sum / scale, (1,))
    d_bias = jnp.reshape(bias_sum / scale, (1,))
    return (loss, d_log_temp, d_bias, grad_images, grad_texts)
```

```python
import jax
import jax.numpy as jnp
from jax import lax
from jax.sharding import Mesh, PartitionSpec as P

AXES = ("y", "z_lo", "x", "z_hi", "core")
SIZES = (8, 8, 4, 2, 2)
LENGTH = {"y": 8, "x": 4, "z": 16, "core": 2}
HIGH = lax.Precision.HIGH


def normalize(x):
    norm = jnp.sqrt(jnp.sum(x * x, axis=1, keepdims=True) + 1e-06)
    return (x / norm, norm)


def unnormalize(unit, norm, grad_unit):
    inner = jnp.sum(unit * grad_unit, axis=1, keepdims=True)
    return (grad_unit - unit * inner) / norm


def place(axis, i):
    return (i % 8) * 2 + i // 8 if axis == "z" else i


def recv(v, axis, step):
    n = LENGTH[axis]
    pairs = [(place(axis, (i + step) % n), place(axis, i)) for i in range(n)]
    return lax.ppermute(v, ("z_lo", "z_hi") if axis == "z" else axis, pairs)


def send(v, axis, step):
    return recv(v, axis, -step)


def cat(*parts):
    return jnp.concatenate(parts, axis=0)


def gather_all(img, txt):
    zp4, zm4 = recv(txt, "z", 4), recv(txt, "z", -4)
    yp2, ym2 = recv(img, "y", 2), recv(img, "y", -2)
    z8 = recv(txt, "z", 8)
    y4 = recv(img, "y", 4)
    even_up, even_down = cat(txt, zp4), cat(txt, zm4)
    zp2, zm2 = recv(even_up, "z", 2), recv(even_down, "z", -2)
    yp1, ym1 = recv(cat(img, yp2), "y", 1), recv(cat(img, ym2), "y", -1)
    zp1 = recv(cat(even_up, zp2), "z", 1)
    zm1 = recv(cat(even_down, zm2), "z", -1)
    line = cat(img, yp2, ym2, y4, yp1, ym1)
    half = line.shape[0] // 2
    xp, xm = recv(line, "x", 1), recv(line, "x", -1)
    own = cat(even_up, zp2, zm4, zm2, z8, zp1, zm1)
    other = recv(own, "core", 1)
    x2a, x2b = recv(xp[:half], "x", 1), recv(xm[half:], "x", -1)
    return (cat(line, xp, xm, x2a, x2b), cat(own, other))


def scatter_img(g, b):
    line, xp, xm, x2a, x2b = g[: 8 * b], g[8 * b : 16 * b], g[16 * b : 24 * b], g[24 * b : 28 * b], g[28 * b :]
    from_m, from_p = send(x2a, "x", 1), send(x2b, "x", -1)
    xp = cat(xp[: 4 * b] + from_m, xp[4 * b :])
    xm = cat(xm[: 4 * b], xm[4 * b :] + from_p)
    line = line + send(xp, "x", 1) + send(xm, "x", -1)
    own, yp2, ym2, y4 = (line[i * b : (i + 1) * b] for i in range(4))
    up, down = send(line[4 * b : 6 * b], "y", 1), send(line[6 * b :], "y", -1)
    far = send(y4, "y", 4)
    near = send(yp2 + up[b:], "y", 2) + send(ym2 + down[b:], "y", -2)
    return own + up[:b] + down[:b] + far + near


def scatter_txt(g, b):
    own = g[: 16 * b] + send(g[16 * b :], "core", 1)
    t0, zp4, zp2, zp6, zm4, zm2, zm6, z8 = (own[i * b : (i + 1) * b] for i in range(8))
    up, down = send(own[8 * b : 12 * b], "z", 1), send(own[12 * b :], "z", -1)
    far = send(z8, "z", 8)
    up2 = send(cat(zp2, zp6) + up[2 * b :], "z", 2)
    down2 = send(cat(zm2, zm6) + down[2 * b :], "z", -2)
    up4 = send(zp4 + up[b : 2 * b] + up2[b:], "z", 4)
    down4 = send(zm4 + down[b : 2 * b] + down2[b:], "z", -4)
    return t0 + up[:b] + down[:b] + up2[:b] + down2[:b] + up4 + down4 + far


def all_sum(parts):
    lanes = jnp.concatenate([jnp.full((8, 128), p, jnp.float32) for p in parts], axis=0)
    for axes in (("z_lo", "z_hi", "core"), ("y", "x")):
        spread = jnp.broadcast_to(lanes, (32,) + lanes.shape)
        lanes = jnp.sum(lax.all_to_all(spread, axes, 0, 0, tiled=True), axis=0)
    return (lanes[0, 0], lanes[8, 0], lanes[16, 0])


def per_device(images, texts, log_temp, bias):
    b = images.shape[0]
    temp = jnp.exp(log_temp[0])
    shift = bias[0]
    unit_img, norm_img = normalize(images)
    unit_txt, norm_txt = normalize(texts)
    img, txt = gather_all(unit_img, unit_txt)
    sim = lax.dot_general(
        img, txt, (((1,), (1,)), ((), ())), precision=HIGH, preferred_element_type=jnp.float32
    )
    logit = temp * sim + shift
    rows = lax.broadcasted_iota(jnp.int32, sim.shape, 0)
    cols = lax.broadcasted_iota(jnp.int32, sim.shape, 1)
    sign = jnp.where((rows == cols) & (rows < b), 1.0, -1.0).astype(jnp.float32)
    pair_grad = -sign * jax.nn.sigmoid(-sign * logit)
    loss_part = jnp.sum(jax.nn.softplus(-sign * logit))
    temp_part = jnp.sum(pair_grad * sim)
    bias_part = jnp.sum(pair_grad)
    grad_img = temp * jnp.dot(pair_grad, txt, precision=HIGH, preferred_element_type=jnp.float32)
    grad_txt = temp * lax.dot_general(
        pair_grad, img, (((0,), (0,)), ((), ())), precision=HIGH, preferred_element_type=jnp.float32
    )
    grad_unit_img = scatter_img(grad_img, b)
    grad_unit_txt = scatter_txt(grad_txt, b)
    loss_all, temp_all, bias_all = all_sum((loss_part, temp_part, bias_part))
    total_rows = jnp.float32(b * 1024)
    loss = jnp.reshape(loss_all / total_rows, (1,))
    d_log_temp = jnp.reshape(temp * temp_all / total_rows, (1,))
    d_bias = jnp.reshape(bias_all / total_rows, (1,))
    grad_images = unnormalize(unit_img, norm_img, grad_unit_img)
    grad_texts = unnormalize(unit_txt, norm_txt, grad_unit_txt)
    return (loss, d_log_temp, d_bias, grad_images, grad_texts)


def solution(mesh):
    fine = Mesh(mesh.devices.reshape(SIZES), AXES)
    rows = P(AXES, None)
    return jax.shard_map(
        per_device, mesh=fine, in_specs=(rows, rows, P(), P()), out_specs=(P(), P(), P(), rows, rows), check_vma=False
    )
```

```python
import jax
import jax.numpy as jnp
from jax import lax
from jax.sharding import Mesh, PartitionSpec as P

AXES = ("y", "z_lo", "x", "z_hi", "core")
SIZES = (8, 8, 4, 2, 2)
PLANE = ("y", "x")
DEPTH = ("z_lo", "z_hi")
HIGH = lax.Precision.HIGH


def normalize(x):
    norm = jnp.sqrt(jnp.sum(x * x, axis=1, keepdims=True) + 1e-06)
    return (x / norm, norm)


def unnormalize(unit, norm, grad_unit):
    inner = jnp.sum(unit * grad_unit, axis=1, keepdims=True)
    return (grad_unit - unit * inner) / norm


def recv(v, axis, step):
    if axis == "core":
        return lax.ppermute(v, axis, [(0, 1), (1, 0)])
    place = lambda z: (z % 8) * 2 + z // 8
    return lax.ppermute(v, DEPTH, [(place((z + step) % 16), place(z)) for z in range(16)])


def send(v, axis, step):
    return recv(v, axis, -step)


def cat(*parts):
    return jnp.concatenate(parts, axis=0)


def gather_txt(txt):
    zp4, zm4 = recv(txt, "z", 4), recv(txt, "z", -4)
    z8 = recv(txt, "z", 8)
    even_up, even_down = cat(txt, zp4), cat(txt, zm4)
    zp2, zm2 = recv(even_up, "z", 2), recv(even_down, "z", -2)
    zp1 = recv(cat(even_up, zp2), "z", 1)
    zm1 = recv(cat(even_down, zm2), "z", -1)
    own = cat(even_up, zp2, zm4, zm2, z8, zp1, zm1)
    return cat(own, recv(own, "core", 1))


def scatter_txt(g, b):
    own = g[: 16 * b] + send(g[16 * b :], "core", 1)
    t0, zp4, zp2, zp6, zm4, zm2, zm6, z8 = (own[i * b : (i + 1) * b] for i in range(8))
    up, down = send(own[8 * b : 12 * b], "z", 1), send(own[12 * b :], "z", -1)
    far = send(z8, "z", 8)
    up2 = send(cat(zp2, zp6) + up[2 * b :], "z", 2)
    down2 = send(cat(zm2, zm6) + down[2 * b :], "z", -2)
    up4 = send(zp4 + up[b : 2 * b] + up2[b:], "z", 4)
    down4 = send(zm4 + down[b : 2 * b] + down2[b:], "z", -4)
    return t0 + up[:b] + down[:b] + up2[:b] + down2[:b] + up4 + down4 + far


def exchange(v, axes):
    return lax.all_to_all(v, axes, 0, 0, tiled=True)


def gather(v, axes):
    n = lax.axis_size(axes)
    return exchange(jnp.broadcast_to(v[None], (n,) + v.shape).reshape(n * v.shape[0], -1), axes)


def scatter(g, axes):
    n = lax.axis_size(axes)
    return jnp.sum(exchange(g, axes).reshape(n, g.shape[0] // n, -1), axis=0)


def pack(parts):
    row = lax.broadcasted_iota(jnp.int32, (8, 128), 0)
    return sum(jnp.where(row == i, p, 0.0) for i, p in enumerate(parts))


def spread_sum(v, axes):
    n = lax.axis_size(axes)
    return jnp.sum(lax.all_to_all(jnp.broadcast_to(v[None], (n,) + v.shape), axes, 0, 0, tiled=True), axis=0)


def per_device(images, texts, log_temp, bias):
    b = images.shape[0]
    temp = jnp.exp(log_temp[0])
    shift = bias[0]
    unit_img, norm_img = normalize(images)
    unit_txt, norm_txt = normalize(texts)
    img = gather(unit_img, PLANE)
    txt = gather_txt(unit_txt)
    first_row = lax.axis_index(PLANE) * b
    sim = lax.dot_general(
        img, txt, (((1,), (1,)), ((), ())), precision=HIGH, preferred_element_type=jnp.float32
    )
    logit = temp * sim + shift
    rows = lax.broadcasted_iota(jnp.int32, sim.shape, 0) - first_row
    cols = lax.broadcasted_iota(jnp.int32, sim.shape, 1)
    sign = jnp.where((rows == cols) & (cols < b), 1.0, -1.0).astype(jnp.float32)
    pair_grad = -sign * jax.nn.sigmoid(-sign * logit)
    loss_part = jnp.sum(jax.nn.softplus(-sign * logit))
    temp_part = jnp.sum(pair_grad * sim)
    bias_part = jnp.sum(pair_grad)
    sums = spread_sum(pack((loss_part, temp_part, bias_part)), DEPTH + ("core",))
    grad_img = temp * jnp.dot(pair_grad, txt, precision=HIGH, preferred_element_type=jnp.float32)
    grad_txt = temp * lax.dot_general(
        pair_grad, img, (((0,), (0,)), ((), ())), precision=HIGH, preferred_element_type=jnp.float32
    )
    sums, grad_img = lax.optimization_barrier((sums, grad_img))
    grad_unit_img = scatter(grad_img, PLANE)
    grad_unit_txt = scatter_txt(grad_txt, b)
    sums, grad_unit_img = lax.optimization_barrier((sums, grad_unit_img))
    sums = spread_sum(sums, PLANE)
    loss_all, temp_all, bias_all = (sums[i, 0] for i in range(3))
    total_rows = jnp.float32(b * 1024)
    loss = jnp.reshape(loss_all / total_rows, (1,))
    d_log_temp = jnp.reshape(temp * temp_all / total_rows, (1,))
    d_bias = jnp.reshape(bias_all / total_rows, (1,))
    grad_images = unnormalize(unit_img, norm_img, grad_unit_img)
    grad_texts = unnormalize(unit_txt, norm_txt, grad_unit_txt)
    return (loss, d_log_temp, d_bias, grad_images, grad_texts)


def solution(mesh):
    fine = Mesh(mesh.devices.reshape(SIZES), AXES)
    rows = P(AXES, None)
    return jax.shard_map(
        per_device, mesh=fine, in_specs=(rows, rows, P(), P()), out_specs=(P(), P(), P(), rows, rows), check_vma=False
    )
```

```python
import jax
import jax.numpy as jnp
from jax import lax
from jax.sharding import Mesh, PartitionSpec as P

AXES = ("y", "z_lo", "x", "z_hi", "core")
SIZES = (8, 8, 4, 2, 2)
PLANE = ("y", "x")
DEPTH = ("z_lo", "z_hi")
HIGH = lax.Precision.HIGH


def normalize(x):
    norm = jnp.sqrt(jnp.sum(x * x, axis=1, keepdims=True) + 1e-06)
    return (x / norm, norm)


def unnormalize(unit, norm, grad_unit):
    inner = jnp.sum(unit * grad_unit, axis=1, keepdims=True)
    return (grad_unit - unit * inner) / norm


def recv(v, axis, step):
    if axis == "core":
        return lax.ppermute(v, axis, [(0, 1), (1, 0)])
    place = lambda z: (z % 8) * 2 + z // 8
    return lax.ppermute(v, DEPTH, [(place((z + step) % 16), place(z)) for z in range(16)])


def send(v, axis, step):
    return recv(v, axis, -step)


def cat(*parts):
    return jnp.concatenate(parts, axis=0)


def gather_txt(txt):
    zp4, zm4 = recv(txt, "z", 4), recv(txt, "z", -4)
    z8 = recv(zp4, "z", 4)
    even_up, even_down = cat(txt, zp4), cat(txt, zm4)
    zp2, zm2 = recv(even_up, "z", 2), recv(even_down, "z", -2)
    zp1 = recv(cat(even_up, zp2), "z", 1)
    zm1 = recv(cat(even_down, zm2), "z", -1)
    own = cat(even_up, zp2, zm4, zm2, z8, zp1, zm1)
    return cat(own, recv(own, "core", 1))


def scatter_txt(g, s, b):
    from_core = send(cat(g[16 * b :], s), "core", 1)
    own, s = g[: 16 * b] + from_core[: 16 * b], s + from_core[16 * b :]
    t0, zp4, zp2, zp6, zm4, zm2, zm6, z8 = (own[i * b : (i + 1) * b] for i in range(8))
    far = send(cat(z8, s), "z", 4)
    up, down = send(cat(own[8 * b : 12 * b], s), "z", 1), send(cat(own[12 * b :], s), "z", -1)
    far, up, down = lax.optimization_barrier((far, up, down))
    below, above = s + up[4 * b :], down[4 * b :]
    up2 = send(cat(cat(zp2, zp6) + up[2 * b : 4 * b], below), "z", 2)
    down2 = send(cat(cat(zm2, zm6) + down[2 * b : 4 * b], s + above), "z", -2)
    below, above = below + up2[2 * b :], above + down2[2 * b :]
    up4 = send(cat(zp4 + far[:b] + up[b : 2 * b] + up2[b : 2 * b], below + far[b:]), "z", 4)
    down4 = send(cat(zm4 + down[b : 2 * b] + down2[b : 2 * b], s + above), "z", -4)
    total = t0 + up[:b] + down[:b] + up2[:b] + down2[:b] + up4[:b] + down4[:b]
    return (total, below + above + up4[b:] + down4[b:])


def exchange(v, axes):
    return lax.all_to_all(v, axes, 0, 0, tiled=True)


def gather(v, axes):
    n = lax.axis_size(axes)
    return exchange(jnp.broadcast_to(v[None], (n,) + v.shape).reshape(n * v.shape[0], -1), axes)


def scatter(g, axes):
    n = lax.axis_size(axes)
    return jnp.sum(exchange(g, axes).reshape(n, g.shape[0] // n, -1), axis=0)


def pack(parts, width):
    row = lax.broadcasted_iota(jnp.int32, (8, width), 0)
    return sum(jnp.where(row == i, p, 0.0) for i, p in enumerate(parts))


def spread_sum(v, axes):
    n = lax.axis_size(axes)
    return jnp.sum(lax.all_to_all(jnp.broadcast_to(v[None], (n,) + v.shape), axes, 0, 0, tiled=True), axis=0)


def per_device(images, texts, log_temp, bias):
    b = images.shape[0]
    temp = jnp.exp(log_temp[0])
    shift = bias[0]
    unit_img, norm_img = normalize(images)
    unit_txt, norm_txt = normalize(texts)
    img = gather(unit_img, PLANE)
    txt = gather_txt(unit_txt)
    first_row = lax.axis_index(PLANE) * b
    sim = lax.dot_general(
        img, txt, (((1,), (1,)), ((), ())), precision=HIGH, preferred_element_type=jnp.float32
    )
    logit = temp * sim + shift
    rows = lax.broadcasted_iota(jnp.int32, sim.shape, 0) - first_row
    cols = lax.broadcasted_iota(jnp.int32, sim.shape, 1)
    sign = jnp.where((rows == cols) & (cols < b), 1.0, -1.0).astype(jnp.float32)
    pair_grad = -sign * jax.nn.sigmoid(-sign * logit)
    loss_part = jnp.sum(jax.nn.softplus(-sign * logit))
    temp_part = jnp.sum(pair_grad * sim)
    bias_part = jnp.sum(pair_grad)
    sums = pack((loss_part, temp_part, bias_part), img.shape[1])
    grad_img = temp * jnp.dot(pair_grad, txt, precision=HIGH, preferred_element_type=jnp.float32)
    pair_grad, grad_img = lax.optimization_barrier((pair_grad, grad_img))
    grad_txt = temp * lax.dot_general(
        pair_grad, img, (((0,), (0,)), ((), ())), precision=HIGH, preferred_element_type=jnp.float32
    )
    grad_unit_img = scatter(grad_img, PLANE)
    grad_unit_txt, sums = scatter_txt(grad_txt, sums, b)
    sums, grad_unit_img = lax.optimization_barrier((sums, grad_unit_img))
    sums = spread_sum(sums[:, :128], PLANE)
    loss_all, temp_all, bias_all = (sums[i, 0] for i in range(3))
    total_rows = jnp.float32(b * 1024)
    loss = jnp.reshape(loss_all / total_rows, (1,))
    d_log_temp = jnp.reshape(temp * temp_all / total_rows, (1,))
    d_bias = jnp.reshape(bias_all / total_rows, (1,))
    grad_images = unnormalize(unit_img, norm_img, grad_unit_img)
    grad_texts = unnormalize(unit_txt, norm_txt, grad_unit_txt)
    return (loss, d_log_temp, d_bias, grad_images, grad_texts)


def solution(mesh):
    fine = Mesh(mesh.devices.reshape(SIZES), AXES)
    rows = P(AXES, None)
    return jax.shard_map(
        per_device, mesh=fine, in_specs=(rows, rows, P(), P()), out_specs=(P(), P(), P(), rows, rows), check_vma=False
    )
```

```python
import jax
import jax.numpy as jnp
from jax import lax
from jax.sharding import Mesh, PartitionSpec as P

AXES = ("y", "z_lo", "x", "z_hi", "core")
SIZES = (8, 8, 4, 2, 2)
PLANE = ("y", "x")
DEPTH = ("z_lo", "z_hi")
HIGH = lax.Precision.HIGH


def normalize(x):
    norm = jnp.sqrt(jnp.sum(x * x, axis=1, keepdims=True) + 1e-06)
    return (x / norm, norm)


def unnormalize(unit, norm, grad_unit):
    inner = jnp.sum(unit * grad_unit, axis=1, keepdims=True)
    return (grad_unit - unit * inner) / norm


def place(z, core):
    return ((z % 8) * 2 + z // 8) * 2 + core


def recv(v, step):
    pairs = []
    for core in range(2):
        for z in range(16):
            pairs.append((place((z + (step if core == 0 else -step)) % 16, core), place(z, core)))
    return lax.ppermute(v, DEPTH + ("core",), pairs)


def send(v, step):
    return recv(v, -step)


def swap_core(v):
    return lax.ppermute(v, "core", [(0, 1), (1, 0)])


def cat(*parts):
    return jnp.concatenate(parts, axis=0)


def gather_txt(txt):
    for step in (8, 4, 2, 1):
        txt = cat(txt, recv(txt, step))
    return cat(txt, swap_core(txt))


def scatter_txt(g, s):
    for step in (0, 1, 2, 4, 8):
        half = g.shape[0] // 2
        message = cat(g[half:], s)
        came = send(message, step) if step else swap_core(message)
        g, s = g[:half] + came[:half], s + came[half:]
    return (g, s)


def exchange(v, axes):
    return lax.all_to_all(v, axes, 0, 0, tiled=True)


def gather(v, axes):
    n = lax.axis_size(axes)
    return exchange(jnp.broadcast_to(v[None], (n,) + v.shape).reshape(n * v.shape[0], -1), axes)


def scatter(g, axes):
    n = lax.axis_size(axes)
    return jnp.sum(exchange(g, axes).reshape(n, g.shape[0] // n, -1), axis=0)


def pack(parts, width):
    row = lax.broadcasted_iota(jnp.int32, (8, width), 0)
    return sum(jnp.where(row == i, p, 0.0) for i, p in enumerate(parts))


def spread_sum(v, axes):
    n = lax.axis_size(axes)
    return jnp.sum(lax.all_to_all(jnp.broadcast_to(v[None], (n,) + v.shape), axes, 0, 0, tiled=True), axis=0)


def per_device(images, texts, log_temp, bias):
    b = images.shape[0]
    temp = jnp.exp(log_temp[0])
    shift = bias[0]
    unit_img, norm_img = normalize(images)
    unit_txt, norm_txt = normalize(texts)
    img = gather(unit_img, PLANE)
    txt = gather_txt(unit_txt)
    first_row = lax.axis_index(PLANE) * b
    sim = lax.dot_general(
        img, txt, (((1,), (1,)), ((), ())), precision=HIGH, preferred_element_type=jnp.float32
    )
    logit = temp * sim + shift
    rows = lax.broadcasted_iota(jnp.int32, sim.shape, 0) - first_row
    cols = lax.broadcasted_iota(jnp.int32, sim.shape, 1)
    sign = jnp.where((rows == cols) & (cols < b), 1.0, -1.0).astype(jnp.float32)
    pair_grad = -sign * jax.nn.sigmoid(-sign * logit)
    loss_part = jnp.sum(jax.nn.softplus(-sign * logit))
    temp_part = jnp.sum(pair_grad * sim)
    bias_part = jnp.sum(pair_grad)
    sums = pack((loss_part, temp_part, bias_part), img.shape[1])
    grad_img = temp * jnp.dot(pair_grad, txt, precision=HIGH, preferred_element_type=jnp.float32)
    pair_grad, grad_img = lax.optimization_barrier((pair_grad, grad_img))
    grad_txt = temp * lax.dot_general(
        pair_grad, img, (((0,), (0,)), ((), ())), precision=HIGH, preferred_element_type=jnp.float32
    )
    grad_unit_img = scatter(grad_img, PLANE)
    grad_unit_txt, sums = scatter_txt(grad_txt, sums)
    sums, grad_unit_img = lax.optimization_barrier((sums, grad_unit_img))
    sums = spread_sum(sums[:, :128], PLANE)
    loss_all, temp_all, bias_all = (sums[i, 0] for i in range(3))
    total_rows = jnp.float32(b * 1024)
    loss = jnp.reshape(loss_all / total_rows, (1,))
    d_log_temp = jnp.reshape(temp * temp_all / total_rows, (1,))
    d_bias = jnp.reshape(bias_all / total_rows, (1,))
    grad_images = unnormalize(unit_img, norm_img, grad_unit_img)
    grad_texts = unnormalize(unit_txt, norm_txt, grad_unit_txt)
    return (loss, d_log_temp, d_bias, grad_images, grad_texts)


def solution(mesh):
    fine = Mesh(mesh.devices.reshape(SIZES), AXES)
    rows = P(AXES, None)
    return jax.shard_map(
        per_device, mesh=fine, in_specs=(rows, rows, P(), P()), out_specs=(P(), P(), P(), rows, rows), check_vma=False
    )
```

```python
import functools

import jax
import jax.numpy as jnp
from jax import lax
from jax.experimental import pallas as pl
from jax.experimental.pallas import tpu as pltpu
from jax.sharding import Mesh, PartitionSpec as P

AXES = ("y", "z_lo", "x", "z_hi", "core")
SIZES = (8, 8, 4, 2, 2)
PLANE = ("y", "x")
DEPTH = ("z_lo", "z_hi")


def normalize(x):
    norm = jnp.sqrt(jnp.sum(x * x, axis=1, keepdims=True) + 1e-06)
    return (x / norm, norm)


def unnormalize(unit, norm, grad_unit):
    inner = jnp.sum(unit * grad_unit, axis=1, keepdims=True)
    return (grad_unit - unit * inner) / norm


def place(z, core):
    return ((z % 8) * 2 + z // 8) * 2 + core


def recv(v, step):
    pairs = []
    for core in range(2):
        for z in range(16):
            pairs.append((place((z + (step if core == 0 else -step)) % 16, core), place(z, core)))
    return lax.ppermute(v, DEPTH + ("core",), pairs)


def send(v, step):
    return recv(v, -step)


def swap_core(v):
    return lax.ppermute(v, "core", [(0, 1), (1, 0)])


def cat(*parts):
    return jnp.concatenate(parts, axis=0)


BROUGHT = (0, 4, 2, 6, -4, -2, -6, 8, 1, 5, 3, 7, -1, -5, -3, -7)
HALVED = (0, 8, 4, -4, 2, -6, 6, -2, 1, -7, 5, -3, 3, -5, 7, -1)


def gather_txt(txt):
    p4, m4 = recv(txt, 4), recv(txt, -4)
    even_up, even_down = cat(txt, p4), cat(txt, m4)
    p2, m2 = recv(even_up, 2), recv(even_down, -2)
    far = recv(p4, 4)
    p1, m1 = recv(cat(even_up, p2), 1), recv(cat(even_down, m2), -1)
    own = cat(even_up, p2, m4, m2, far, p1, m1)
    return (own, swap_core(own))


def scatter_txt(g, s):
    for step in (0, 1, 2, 4, 8):
        half = g.shape[0] // 2
        message = cat(g[half:], s)
        came = send(message, step) if step else swap_core(message)
        g, s = g[:half] + came[:half], s + came[half:]
    return (g, s)


def exchange(v, axes):
    return lax.all_to_all(v, axes, 0, 0, tiled=True)


def gather(v, axes):
    n = lax.axis_size(axes)
    return exchange(jnp.broadcast_to(v[None], (n,) + v.shape).reshape(n * v.shape[0], -1), axes)


def scatter(g, axes):
    n = lax.axis_size(axes)
    return jnp.sum(exchange(g, axes).reshape(n, g.shape[0] // n, -1), axis=0)


def split(x):
    hi = x.astype(jnp.bfloat16)
    return (hi, (x - hi.astype(jnp.float32)).astype(jnp.bfloat16))


def dot3(a, b, dims):
    def dot(x, y):
        return lax.dot_general(x, y, (dims, ((), ())), preferred_element_type=jnp.float32)

    return dot(a[0], b[0]) + (dot(a[0], b[1]) + dot(a[1], b[0]))


def tile_kernel(b, scal, first, img, own, other, grad_img, grad_txt, sums, txt_hi, txt_lo):
    temp, shift = scal[0], scal[1]
    half = own.shape[0]
    for part, ref in enumerate((own, other)):
        for to, z in enumerate(HALVED):
            at = BROUGHT.index(z) * b
            hi, lo = split(ref[at : at + b, :])
            start = part * half + to * b
            txt_hi[start : start + b, :] = hi
            txt_lo[start : start + b, :] = lo
    txt = (txt_hi[...], txt_lo[...])
    chunk = img.shape[0] // 2
    totals = [jnp.float32(0)] * 3
    for k in range(2):
        part = split(img[k * chunk : (k + 1) * chunk, :])
        sim = dot3(part, txt, ((1,), (1,)))
        logit = temp * sim + shift
        rows = lax.broadcasted_iota(jnp.int32, sim.shape, 0) + (k * chunk - first[0])
        cols = lax.broadcasted_iota(jnp.int32, sim.shape, 1)
        same = (rows == cols) & (cols < b)
        x = jnp.where(same, -logit, logit)
        e = jnp.exp(-jnp.abs(x))
        sig = jnp.where(x >= 0, 1.0, e) / (1.0 + e)
        pair = jnp.where(same, -sig, sig)
        totals[0] += jnp.sum(jnp.maximum(x, 0.0) + jnp.log1p(e))
        totals[1] += jnp.sum(pair * sim)
        totals[2] += jnp.sum(pair)
        pair = split(pair)
        grad_img[k * chunk : (k + 1) * chunk, :] = temp * dot3(pair, txt, ((1,), (0,)))
        term = temp * dot3(pair, part, ((0,), (0,)))
        grad_txt[...] = term if k == 0 else grad_txt[...] + term
    row = lax.broadcasted_iota(jnp.int32, sums.shape, 0)
    sums[...] = jnp.where(row == 0, totals[0], jnp.where(row == 1, totals[1], totals[2]))


def tile_terms(scal, first, img, own, other, b):
    n, d = img.shape
    m = 2 * own.shape[0]
    smem, vmem = pl.BlockSpec(memory_space=pltpu.SMEM), pl.BlockSpec(memory_space=pltpu.VMEM)
    return pl.pallas_call(
        functools.partial(tile_kernel, b),
        out_shape=(
            jax.ShapeDtypeStruct((n, d), jnp.float32),
            jax.ShapeDtypeStruct((m, d), jnp.float32),
            jax.ShapeDtypeStruct((8, 128), jnp.float32),
        ),
        in_specs=[smem, smem, vmem, vmem, vmem],
        out_specs=(vmem, vmem, vmem),
        scratch_shapes=[pltpu.VMEM((m, d), jnp.bfloat16), pltpu.VMEM((m, d), jnp.bfloat16)],
        compiler_params=pltpu.CompilerParams(vmem_limit_bytes=40 * 1024 * 1024),
        cost_estimate=pl.CostEstimate(flops=18 * n * m * d, bytes_accessed=8 * (n + m) * d, transcendentals=3 * n * m),
        name="pair_tile",
    )(scal, first, img, own, other)


def spread_sum(v, axes):
    n = lax.axis_size(axes)
    return jnp.sum(lax.all_to_all(jnp.broadcast_to(v[None], (n,) + v.shape), axes, 0, 0, tiled=True), axis=0)


def per_device(images, texts, log_temp, bias):
    b = images.shape[0]
    temp = jnp.exp(log_temp[0])
    shift = bias[0]
    unit_img, norm_img = normalize(images)
    unit_txt, norm_txt = normalize(texts)
    img = gather(unit_img, PLANE)
    own, other = gather_txt(unit_txt)
    first_row = jnp.reshape(lax.axis_index(PLANE) * b, (1,)).astype(jnp.int32)
    grad_img, grad_txt, sums = tile_terms(jnp.stack([temp, shift]), first_row, img, own, other, b)
    sums = jnp.pad(sums, ((0, 0), (0, img.shape[1] - 128)))
    grad_unit_img = scatter(grad_img, PLANE)
    grad_unit_txt, sums = scatter_txt(grad_txt, sums)
    sums, grad_unit_img = lax.optimization_barrier((sums, grad_unit_img))
    sums = spread_sum(spread_sum(sums[:, :128], "y"), "x")
    loss_all, temp_all, bias_all = (sums[i, 0] for i in range(3))
    total_rows = jnp.float32(b * 1024)
    loss = jnp.reshape(loss_all / total_rows, (1,))
    d_log_temp = jnp.reshape(temp * temp_all / total_rows, (1,))
    d_bias = jnp.reshape(bias_all / total_rows, (1,))
    grad_images = unnormalize(unit_img, norm_img, grad_unit_img)
    grad_texts = unnormalize(unit_txt, norm_txt, grad_unit_txt)
    return (loss, d_log_temp, d_bias, grad_images, grad_texts)


def solution(mesh):
    fine = Mesh(mesh.devices.reshape(SIZES), AXES)
    rows = P(AXES, None)
    return jax.shard_map(
        per_device, mesh=fine, in_specs=(rows, rows, P(), P()), out_specs=(P(), P(), P(), rows, rows), check_vma=False
    )
```

```python
import functools

import jax
import jax.numpy as jnp
from jax import lax
from jax.experimental import pallas as pl
from jax.experimental.pallas import tpu as pltpu
from jax.sharding import Mesh, PartitionSpec as P

AXES = ("y", "z_lo", "x", "z_hi", "core")
SIZES = (8, 8, 4, 2, 2)
PLANE = ("y", "x")
DEPTH = ("z_lo", "z_hi")


def normalize(x):
    norm = jnp.sqrt(jnp.sum(x * x, axis=1, keepdims=True) + 1e-06)
    return (x / norm, norm)


def unnormalize(unit, norm, grad_unit):
    inner = jnp.sum(unit * grad_unit, axis=1, keepdims=True)
    return (grad_unit - unit * inner) / norm


def place(z, core):
    return ((z % 8) * 2 + z // 8) * 2 + core


def recv(v, step):
    pairs = []
    for core in range(2):
        for z in range(16):
            pairs.append((place((z + (step if core == 0 else -step)) % 16, core), place(z, core)))
    return lax.ppermute(v, DEPTH + ("core",), pairs)


def send(v, step):
    return recv(v, -step)


def swap_core(v):
    return lax.ppermute(v, "core", [(0, 1), (1, 0)])


def cat(*parts):
    return jnp.concatenate(parts, axis=0)


BROUGHT = (0, 4, 2, 6, -4, -2, -6, 8, 1, 5, 3, 7, -1, -5, -3, -7)
HALVED = (0, 8, 4, -4, 2, -6, 6, -2, 1, -7, 5, -3, 3, -5, 7, -1)


def gather_txt(txt):
    p4, m4 = recv(txt, 4), recv(txt, -4)
    even_up, even_down = cat(txt, p4), cat(txt, m4)
    p2, m2 = recv(even_up, 2), recv(even_down, -2)
    far = recv(p4, 4)
    p1, m1 = recv(cat(even_up, p2), 1), recv(cat(even_down, m2), -1)
    own = cat(even_up, p2, m4, m2, far, p1, m1)
    return (own, swap_core(own))


def scatter_txt(g, s):
    lanes = s.shape[1]
    s = jnp.pad(s, ((0, 0), (0, g.shape[1] - lanes)))
    for step in (0, 1):
        half = g.shape[0] // 2
        message = cat(g[half:], s)
        came = send(message, step) if step else swap_core(message)
        g, s = g[:half] + came[:half], s + came[half:]
    s = s[:, :lanes]
    beside = {2: (("z", 2), ("z", 4), ("z", 8)), 4: (("y", 1), ("y", 2)), 8: (("y", 4), ("x", 1), ("x", 2))}
    for step, small in beside.items():
        half = g.shape[0] // 2
        came = send(g[half:], step)
        for axis, by in small:
            s = s + (send(s, by) if axis == "z" else shift(s, axis, by))
        g = g[:half] + came
        g, s = lax.optimization_barrier((g, s))
    return (g, s)


def shift(s, axis, step):
    n = lax.axis_size(axis)
    return lax.ppermute(s, axis, [(i, (i + step) % n) for i in range(n)])


def exchange(v, axes):
    return lax.all_to_all(v, axes, 0, 0, tiled=True)


def gather(v, axes):
    n = lax.axis_size(axes)
    return exchange(jnp.broadcast_to(v[None], (n,) + v.shape).reshape(n * v.shape[0], -1), axes)


def scatter(g, axes):
    n = lax.axis_size(axes)
    return jnp.sum(exchange(g, axes).reshape(n, g.shape[0] // n, -1), axis=0)


def split(x):
    hi = x.astype(jnp.bfloat16)
    return (hi, (x - hi.astype(jnp.float32)).astype(jnp.bfloat16))


def dot3(a, b, dims):
    def dot(x, y):
        return lax.dot_general(x, y, (dims, ((), ())), preferred_element_type=jnp.float32)

    return dot(a[0], b[0]) + (dot(a[0], b[1]) + dot(a[1], b[0]))


def tile_kernel(b, scal, first, img, own, other, grad_img, grad_txt, sums, txt_hi, txt_lo):
    temp, shift = scal[0], scal[1]
    half = own.shape[0]
    for part, ref in enumerate((own, other)):
        for to, z in enumerate(HALVED):
            at = BROUGHT.index(z) * b
            hi, lo = split(ref[at : at + b, :])
            start = part * half + to * b
            txt_hi[start : start + b, :] = hi
            txt_lo[start : start + b, :] = lo
    txt = (txt_hi[...], txt_lo[...])
    chunk = img.shape[0] // 2
    totals = [jnp.float32(0)] * 3
    for k in range(2):
        part = split(img[k * chunk : (k + 1) * chunk, :])
        sim = dot3(part, txt, ((1,), (1,)))
        logit = temp * sim + shift
        rows = lax.broadcasted_iota(jnp.int32, sim.shape, 0) + (k * chunk - first[0])
        cols = lax.broadcasted_iota(jnp.int32, sim.shape, 1)
        same = (rows == cols) & (cols < b)
        x = jnp.where(same, -logit, logit)
        e = jnp.exp(-jnp.abs(x))
        sig = jnp.where(x >= 0, 1.0, e) / (1.0 + e)
        pair = jnp.where(same, -sig, sig)
        totals[0] += jnp.sum(jnp.maximum(x, 0.0) + jnp.log1p(e))
        totals[1] += jnp.sum(pair * sim)
        totals[2] += jnp.sum(pair)
        pair = split(pair)
        grad_img[k * chunk : (k + 1) * chunk, :] = temp * dot3(pair, txt, ((1,), (0,)))
        term = temp * dot3(pair, part, ((0,), (0,)))
        grad_txt[...] = term if k == 0 else grad_txt[...] + term
    row = lax.broadcasted_iota(jnp.int32, sums.shape, 0)
    sums[...] = jnp.where(row == 0, totals[0], jnp.where(row == 1, totals[1], totals[2]))


def tile_terms(scal, first, img, own, other, b):
    n, d = img.shape
    m = 2 * own.shape[0]
    smem, vmem = pl.BlockSpec(memory_space=pltpu.SMEM), pl.BlockSpec(memory_space=pltpu.VMEM)
    return pl.pallas_call(
        functools.partial(tile_kernel, b),
        out_shape=(
            jax.ShapeDtypeStruct((n, d), jnp.float32),
            jax.ShapeDtypeStruct((m, d), jnp.float32),
            jax.ShapeDtypeStruct((8, 128), jnp.float32),
        ),
        in_specs=[smem, smem, vmem, vmem, vmem],
        out_specs=(vmem, vmem, vmem),
        scratch_shapes=[pltpu.VMEM((m, d), jnp.bfloat16), pltpu.VMEM((m, d), jnp.bfloat16)],
        compiler_params=pltpu.CompilerParams(vmem_limit_bytes=40 * 1024 * 1024),
        cost_estimate=pl.CostEstimate(flops=18 * n * m * d, bytes_accessed=8 * (n + m) * d, transcendentals=3 * n * m),
        name="pair_tile",
    )(scal, first, img, own, other)


def per_device(images, texts, log_temp, bias):
    b = images.shape[0]
    temp = jnp.exp(log_temp[0])
    shift = bias[0]
    unit_img, norm_img = normalize(images)
    unit_txt, norm_txt = normalize(texts)
    img = gather(unit_img, PLANE)
    own, other = gather_txt(unit_txt)
    first_row = jnp.reshape(lax.axis_index(PLANE) * b, (1,)).astype(jnp.int32)
    grad_img, grad_txt, sums = tile_terms(jnp.stack([temp, shift]), first_row, img, own, other, b)
    grad_unit_img = scatter(grad_img, PLANE)
    grad_unit_txt, sums = scatter_txt(grad_txt, sums)
    loss_all, temp_all, bias_all = (sums[i, 0] for i in range(3))
    total_rows = jnp.float32(b * 1024)
    loss = jnp.reshape(loss_all / total_rows, (1,))
    d_log_temp = jnp.reshape(temp * temp_all / total_rows, (1,))
    d_bias = jnp.reshape(bias_all / total_rows, (1,))
    grad_images = unnormalize(unit_img, norm_img, grad_unit_img)
    grad_texts = unnormalize(unit_txt, norm_txt, grad_unit_txt)
    return (loss, d_log_temp, d_bias, grad_images, grad_texts)


def solution(mesh):
    fine = Mesh(mesh.devices.reshape(SIZES), AXES)
    rows = P(AXES, None)
    return jax.shard_map(
        per_device, mesh=fine, in_specs=(rows, rows, P(), P()), out_specs=(P(), P(), P(), rows, rows), check_vma=False
    )
```

```python
import functools

import jax
import jax.numpy as jnp
from jax import lax
from jax.experimental import pallas as pl
from jax.experimental.pallas import tpu as pltpu
from jax.sharding import Mesh, PartitionSpec as P

AXES = ("y", "z_lo", "x", "z_hi", "core")
SIZES = (8, 8, 4, 2, 2)
PLANE = ("y", "x")
DEPTH = ("z_lo", "z_hi")


def normalize(x):
    norm = jnp.sqrt(jnp.sum(x * x, axis=1, keepdims=True) + 1e-06)
    return (x / norm, norm)


def unnormalize(unit, norm, grad_unit):
    inner = jnp.sum(unit * grad_unit, axis=1, keepdims=True)
    return (grad_unit - unit * inner) / norm


def place(z, core):
    return ((z % 8) * 2 + z // 8) * 2 + core


def recv(v, step):
    pairs = []
    for core in range(2):
        for z in range(16):
            pairs.append((place((z + (step if core == 0 else -step)) % 16, core), place(z, core)))
    return lax.ppermute(v, DEPTH + ("core",), pairs)


def send(v, step):
    return recv(v, -step)


def swap_core(v):
    return lax.ppermute(v, "core", [(0, 1), (1, 0)])


def cat(*parts):
    return jnp.concatenate(parts, axis=0)


BROUGHT = (0, 4, 2, 6, -4, -2, -6, 8, 1, 5, 3, 7, -1, -5, -3, -7)
HALVED = (0, 8, 4, -4, 2, -6, 6, -2, 1, -7, 5, -3, 3, -5, 7, -1)


def gather_txt(txt):
    p4, m4 = recv(txt, 4), recv(txt, -4)
    even_up, even_down = cat(txt, p4), cat(txt, m4)
    p2, m2 = recv(even_up, 2), recv(even_down, -2)
    far = recv(p4, 4)
    p1, m1 = recv(cat(even_up, p2), 1), recv(cat(even_down, m2), -1)
    own = cat(even_up, p2, m4, m2, far, p1, m1)
    return (own, swap_core(own))


def scatter_txt(g, message, b):
    s = message[-8:]
    came = swap_core(message)
    for step in (1, 2):
        g, s = g + came[:-8], s + came[-8:]
        half = g.shape[0] // 2
        came = send(cat(g[half:], s), step)
        g = g[:half]
    g, s = g + came[:-8], s + came[-8:]
    own, z8, p4, m4 = (g[i * b : (i + 1) * b] for i in range(4))
    far = send(cat(z8, s), 4)
    down = send(cat(m4, s), -4)
    up = send(cat(p4 + far[:b], s + far[b:]), 4)
    return (own + up[:b] + down[:b], s + up[b:] + down[b:])


def exchange(v, axes):
    return lax.all_to_all(v, axes, 0, 0, tiled=True)


def gather(v, axes):
    n = lax.axis_size(axes)
    return exchange(jnp.broadcast_to(v[None], (n,) + v.shape).reshape(n * v.shape[0], -1), axes)


def scatter(g, axes):
    n = lax.axis_size(axes)
    return jnp.sum(exchange(g, axes).reshape(n, g.shape[0] // n, -1), axis=0)


def split(x):
    hi = x.astype(jnp.bfloat16)
    return (hi, (x - hi.astype(jnp.float32)).astype(jnp.bfloat16))


def dot3(a, b, dims):
    def dot(x, y):
        return lax.dot_general(x, y, (dims, ((), ())), preferred_element_type=jnp.float32)

    return dot(a[0], b[0]) + (dot(a[0], b[1]) + dot(a[1], b[0]))


def unit_split(x):
    norm = jnp.sqrt(jnp.sum(x * x, axis=1, keepdims=True) + 1e-06)
    return split(x * (1.0 / norm))


def tile_kernel(b, scal, first, img, own, other, grad_img, grad_own, message, txt_hi, txt_lo):
    temp, shift = scal[0], scal[1]
    half = own.shape[0]
    for part, ref in enumerate((own, other)):
        for to, z in enumerate(HALVED):
            at = BROUGHT.index(z) * b
            hi, lo = unit_split(ref[at : at + b, :])
            start = part * half + to * b
            txt_hi[start : start + b, :] = hi
            txt_lo[start : start + b, :] = lo
    txt = (txt_hi[...], txt_lo[...])
    chunk = img.shape[0] // 2
    totals = [jnp.float32(0)] * 3
    for k in range(2):
        part = unit_split(img[k * chunk : (k + 1) * chunk, :])
        sim = dot3(part, txt, ((1,), (1,)))
        logit = temp * sim + shift
        rows = lax.broadcasted_iota(jnp.int32, sim.shape, 0) + (k * chunk - first[0])
        cols = lax.broadcasted_iota(jnp.int32, sim.shape, 1)
        same = (rows == cols) & (cols < b)
        x = jnp.where(same, -logit, logit)
        e = jnp.exp(-jnp.abs(x))
        sig = jnp.where(x >= 0, 1.0, e) / (1.0 + e)
        pair = jnp.where(same, -sig, sig)
        totals[0] += jnp.sum(jnp.maximum(x, 0.0) + jnp.log1p(e))
        totals[1] += jnp.sum(pair * sim)
        totals[2] += jnp.sum(pair)
        pair = split(pair)
        grad_img[k * chunk : (k + 1) * chunk, :] = temp * dot3(pair, txt, ((1,), (0,)))
        term = temp * dot3(pair, part, ((0,), (0,)))
        grad_own[...] = term[:half] if k == 0 else grad_own[...] + term[:half]
        message[:half, :] = term[half:] if k == 0 else message[:half, :] + term[half:]
    row = lax.broadcasted_iota(jnp.int32, (8, img.shape[1]), 0)
    message[half:, :] = jnp.where(row == 0, totals[0], jnp.where(row == 1, totals[1], totals[2]))


def tile_terms(scal, first, img, own, other, b):
    n, d = img.shape
    half = own.shape[0]
    m = 2 * half
    smem, vmem = pl.BlockSpec(memory_space=pltpu.SMEM), pl.BlockSpec(memory_space=pltpu.VMEM)
    return pl.pallas_call(
        functools.partial(tile_kernel, b),
        out_shape=(
            jax.ShapeDtypeStruct((n, d), jnp.float32),
            jax.ShapeDtypeStruct((half, d), jnp.float32),
            jax.ShapeDtypeStruct((half + 8, d), jnp.float32),
        ),
        in_specs=[smem, smem, vmem, vmem, vmem],
        out_specs=(vmem, vmem, vmem),
        scratch_shapes=[pltpu.VMEM((m, d), jnp.bfloat16), pltpu.VMEM((m, d), jnp.bfloat16)],
        compiler_params=pltpu.CompilerParams(vmem_limit_bytes=40 * 1024 * 1024),
        cost_estimate=pl.CostEstimate(flops=18 * n * m * d, bytes_accessed=8 * (n + m) * d, transcendentals=3 * n * m),
        name="pair_tile",
    )(scal, first, img, own, other)


def spread_sum(v, axes):
    n = lax.axis_size(axes)
    return jnp.sum(lax.all_to_all(jnp.broadcast_to(v[None], (n,) + v.shape), axes, 0, 0, tiled=True), axis=0)


def per_device(images, texts, log_temp, bias):
    b = images.shape[0]
    temp = jnp.exp(log_temp[0])
    shift = bias[0]
    own, other = gather_txt(texts)
    img = gather(images, PLANE)
    first_row = jnp.reshape(lax.axis_index(PLANE) * b, (1,)).astype(jnp.int32)
    grad_img, grad_own, message = tile_terms(jnp.stack([temp, shift]), first_row, img, own, other, b)
    grad_unit_img = scatter(grad_img, PLANE)
    grad_unit_txt, sums = scatter_txt(grad_own, message, b)
    sums, grad_unit_img = lax.optimization_barrier((sums, grad_unit_img))
    sums = spread_sum(spread_sum(sums[:, :128], "y"), "x")
    loss_all, temp_all, bias_all = (sums[i, 0] for i in range(3))
    total_rows = jnp.float32(b * 1024)
    loss = jnp.reshape(loss_all / total_rows, (1,))
    d_log_temp = jnp.reshape(temp * temp_all / total_rows, (1,))
    d_bias = jnp.reshape(bias_all / total_rows, (1,))
    unit_img, norm_img = normalize(images)
    unit_txt, norm_txt = normalize(texts)
    grad_images = unnormalize(unit_img, norm_img, grad_unit_img)
    grad_texts = unnormalize(unit_txt, norm_txt, grad_unit_txt)
    return (loss, d_log_temp, d_bias, grad_images, grad_texts)


def solution(mesh):
    fine = Mesh(mesh.devices.reshape(SIZES), AXES)
    rows = P(AXES, None)
    return jax.shard_map(
        per_device, mesh=fine, in_specs=(rows, rows, P(), P()), out_specs=(P(), P(), P(), rows, rows), check_vma=False
    )
```

```python
import functools

import jax
import jax.numpy as jnp
from jax import lax
from jax.experimental import pallas as pl
from jax.experimental.pallas import tpu as pltpu
from jax.sharding import Mesh, PartitionSpec as P

AXES = ("y", "z_lo", "x", "z_hi", "core")
SIZES = (8, 8, 4, 2, 2)
PLANE = ("y", "x")
DEPTH = ("z_lo", "z_hi")


def normalize(x):
    norm = jnp.sqrt(jnp.sum(x * x, axis=1, keepdims=True) + 1e-06)
    return (x / norm, norm)


def unnormalize(unit, norm, grad_unit):
    inner = jnp.sum(unit * grad_unit, axis=1, keepdims=True)
    return (grad_unit - unit * inner) / norm


def place(z, core):
    return ((z % 8) * 2 + z // 8) * 2 + core


def recv(v, step):
    pairs = []
    for core in range(2):
        for z in range(16):
            pairs.append((place((z + (step if core == 0 else -step)) % 16, core), place(z, core)))
    return lax.ppermute(v, DEPTH + ("core",), pairs)


def send(v, step):
    return recv(v, -step)


def swap_core(v):
    return lax.ppermute(v, "core", [(0, 1), (1, 0)])


def cat(*parts):
    return jnp.concatenate(parts, axis=0)


BROUGHT = (0, 4, 2, 6, -4, -2, -6, 8, 1, 5, 3, 7, -1, -5, -3, -7)
HALVED = (0, 8, 4, -4, 2, -6, 6, -2, 1, -7, 5, -3, 3, -5, 7, -1)


def gather_txt(txt):
    p4, m4 = recv(txt, 4), recv(txt, -4)
    even_up, even_down = cat(txt, p4), cat(txt, m4)
    p2, m2 = recv(even_up, 2), recv(even_down, -2)
    far = recv(p4, 4)
    p1, m1 = recv(cat(even_up, p2), 1), recv(cat(even_down, m2), -1)
    own = cat(even_up, p2, m4, m2, far, p1, m1)
    return (own, swap_core(own))


def fold(g, step):
    half = g.shape[0] // 2
    return g[:half] + send(g[half:], step)


def exchange(v, axes):
    return lax.all_to_all(v, axes, 0, 0, tiled=True)


def gather(v, axes):
    n = lax.axis_size(axes)
    return exchange(jnp.broadcast_to(v[None], (n,) + v.shape).reshape(n * v.shape[0], -1), axes)


def split(x):
    hi = x.astype(jnp.bfloat16)
    return (hi, (x - hi.astype(jnp.float32)).astype(jnp.bfloat16))


def dot3(a, b, dims):
    def dot(x, y):
        return lax.dot_general(x, y, (dims, ((), ())), preferred_element_type=jnp.float32)

    return dot(a[0], b[0]) + (dot(a[0], b[1]) + dot(a[1], b[0]))


def tile_kernel(b, scal, first, img, own, other, grad_img, grad_own, message, sums, txt_hi, txt_lo):
    temp, shift = scal[0], scal[1]
    half = own.shape[0]
    wide = img.shape[1] // 128
    for part, ref in enumerate((own, other)):
        for to, z in enumerate(HALVED):
            at = BROUGHT.index(z) * b
            hi, lo = split(ref[at : at + b, :])
            start = part * half + to * b
            txt_hi[start : start + b, :] = hi
            txt_lo[start : start + b, :] = lo
    txt = (txt_hi[...], txt_lo[...])
    chunk = img.shape[0] // 2
    totals = [jnp.float32(0)] * 3
    for k in range(2):
        part = split(img[k * chunk : (k + 1) * chunk, :])
        sim = dot3(part, txt, ((1,), (1,)))
        logit = temp * sim + shift
        rows = lax.broadcasted_iota(jnp.int32, sim.shape, 0) + (k * chunk - first[0])
        cols = lax.broadcasted_iota(jnp.int32, sim.shape, 1)
        same = (rows == cols) & (cols < b)
        x = jnp.where(same, -logit, logit)
        e = jnp.exp(-jnp.abs(x))
        sig = jnp.where(x >= 0, 1.0, e) / (1.0 + e)
        pair = jnp.where(same, -sig, sig)
        totals[0] += jnp.sum(jnp.maximum(x, 0.0) + jnp.log1p(e))
        totals[1] += jnp.sum(pair * sim)
        totals[2] += jnp.sum(pair)
        pair = split(pair)
        term = temp * dot3(pair, txt, ((1,), (0,)))
        for at in range(0, chunk, 8):
            block, tile = (k * chunk + at) // b, (at % b) // 8 * wide
            for j in range(wide):
                grad_img[block, tile + j, :, :] = term[at : at + 8, j * 128 : (j + 1) * 128]
        term = temp * dot3(pair, part, ((0,), (0,)))
        grad_own[...] = term[:half] if k == 0 else grad_own[...] + term[:half]
        message[...] = term[half:] if k == 0 else message[...] + term[half:]
    row = lax.broadcasted_iota(jnp.int32, sums.shape, 0)
    sums[...] = jnp.where(row == 0, totals[0], jnp.where(row == 1, totals[1], totals[2]))


def tile_terms(scal, first, img, own, other, b):
    n, d = img.shape
    half = own.shape[0]
    m = 2 * half
    smem, vmem = pl.BlockSpec(memory_space=pltpu.SMEM), pl.BlockSpec(memory_space=pltpu.VMEM)
    return pl.pallas_call(
        functools.partial(tile_kernel, b),
        out_shape=(
            jax.ShapeDtypeStruct((n // b, b * d // 1024 + 1, 8, 128), jnp.float32),
            jax.ShapeDtypeStruct((half, d), jnp.float32),
            jax.ShapeDtypeStruct((half, d), jnp.float32),
            jax.ShapeDtypeStruct((8, 128), jnp.float32),
        ),
        in_specs=[smem, smem, vmem, vmem, vmem],
        out_specs=(vmem, vmem, vmem, vmem),
        scratch_shapes=[pltpu.VMEM((m, d), jnp.bfloat16), pltpu.VMEM((m, d), jnp.bfloat16)],
        compiler_params=pltpu.CompilerParams(vmem_limit_bytes=40 * 1024 * 1024),
        cost_estimate=pl.CostEstimate(flops=18 * n * m * d, bytes_accessed=8 * (n + m) * d, transcendentals=3 * n * m),
        name="pair_tile",
    )(scal, first, img, own, other)


def spread_sum(v, axes):
    n = lax.axis_size(axes)
    return jnp.sum(lax.all_to_all(jnp.broadcast_to(v[None], (n,) + v.shape), axes, 0, 0, tiled=True), axis=0)


def per_device(images, texts, log_temp, bias):
    b = images.shape[0]
    temp = jnp.exp(log_temp[0])
    shift = bias[0]
    unit_img, norm_img = normalize(images)
    unit_txt, norm_txt = normalize(texts)
    img = gather(unit_img, PLANE)
    own, other = gather_txt(unit_txt)
    first_row = jnp.reshape(lax.axis_index(PLANE) * b, (1,)).astype(jnp.int32)
    tiles, grad_own, message, sums = tile_terms(jnp.stack([temp, shift]), first_row, img, own, other, b)
    grad_txt = fold(grad_own + swap_core(message), 1)
    sums = spread_sum(sums, DEPTH + ("core",))
    sums, grad_txt = lax.optimization_barrier((sums, grad_txt))
    tiles = jnp.sum(exchange(tiles.at[:, -1].set(sums[None]), PLANE), axis=0)
    wide = img.shape[1] // 128
    grad_unit_img = jnp.swapaxes(tiles[:-1].reshape(b // 8, wide, 8, 128), 1, 2).reshape(b, -1)
    sums = tiles[-1]
    grad_unit_txt = fold(fold(fold(grad_txt, 2), 4), 8)
    loss_all, temp_all, bias_all = (sums[i, 0] for i in range(3))
    total_rows = jnp.float32(b * 1024)
    loss = jnp.reshape(loss_all / total_rows, (1,))
    d_log_temp = jnp.reshape(temp * temp_all / total_rows, (1,))
    d_bias = jnp.reshape(bias_all / total_rows, (1,))
    grad_images = unnormalize(unit_img, norm_img, grad_unit_img)
    grad_texts = unnormalize(unit_txt, norm_txt, grad_unit_txt)
    return (loss, d_log_temp, d_bias, grad_images, grad_texts)


def solution(mesh):
    fine = Mesh(mesh.devices.reshape(SIZES), AXES)
    rows = P(AXES, None)
    return jax.shard_map(
        per_device, mesh=fine, in_specs=(rows, rows, P(), P()), out_specs=(P(), P(), P(), rows, rows), check_vma=False
    )
```

```python
import functools

import jax
import jax.numpy as jnp
from jax import lax
from jax.experimental import pallas as pl
from jax.experimental.pallas import tpu as pltpu
from jax.sharding import Mesh, PartitionSpec as P

AXES = ("y", "z_lo", "x", "z_hi", "core")
SIZES = (8, 8, 4, 2, 2)
PLANE = ("y", "x")
DEPTH = ("z_lo", "z_hi")


def normalize(x):
    norm = jnp.sqrt(jnp.sum(x * x, axis=1, keepdims=True) + 1e-06)
    return (x / norm, norm)


def unnormalize(unit, norm, grad_unit):
    inner = jnp.sum(unit * grad_unit, axis=1, keepdims=True)
    return (grad_unit - unit * inner) / norm


def place(z, core):
    return ((z % 8) * 2 + z // 8) * 2 + core


def recv(v, step):
    pairs = []
    for core in range(2):
        for z in range(16):
            pairs.append((place((z + (step if core == 0 else -step)) % 16, core), place(z, core)))
    return lax.ppermute(v, DEPTH + ("core",), pairs)


def send(v, step):
    return recv(v, -step)


def swap_core(v):
    return lax.ppermute(v, "core", [(0, 1), (1, 0)])


def cat(*parts):
    return jnp.concatenate(parts, axis=0)


BROUGHT = (0, 4, 2, 6, -4, -2, -6, 8, 1, 5, 3, 7, -1, -5, -3, -7)
HALVED = (0, 8, 4, -4, 2, -6, 6, -2, 1, -7, 5, -3, 3, -5, 7, -1)


def gather_txt(txt):
    p4, m4 = recv(txt, 4), recv(txt, -4)
    even_up, even_down = cat(txt, p4), cat(txt, m4)
    p2, m2 = recv(even_up, 2), recv(even_down, -2)
    far = recv(p4, 4)
    p1, m1 = recv(cat(even_up, p2), 1), recv(cat(even_down, m2), -1)
    own = cat(even_up, p2, m4, m2, far, p1, m1)
    return (own, swap_core(own))


def fold(g, step):
    half = g.shape[0] // 2
    return g[:half] + send(g[half:], step)


def exchange(v, axes):
    return lax.all_to_all(v, axes, 0, 0, tiled=True)


def gather(v, axes):
    n = lax.axis_size(axes)
    return exchange(jnp.broadcast_to(v[None], (n,) + v.shape).reshape(n * v.shape[0], -1), axes)


def split(x):
    hi = x.astype(jnp.bfloat16)
    return (hi, (x - hi.astype(jnp.float32)).astype(jnp.bfloat16))


def dot3(a, b, dims):
    def dot(x, y):
        return lax.dot_general(x, y, (dims, ((), ())), preferred_element_type=jnp.float32)

    return dot(a[0], b[0]) + (dot(a[0], b[1]) + dot(a[1], b[0]))


def tile_kernel(b, images, scal, first, img, own, other, *refs):
    *outs, txt_hi, txt_lo = refs
    temp, shift = scal[0], scal[1]
    half = own.shape[0]
    wide = img.shape[1] // 128
    for part, ref in enumerate((own, other)):
        for to, z in enumerate(HALVED):
            at = BROUGHT.index(z) * b
            hi, lo = split(ref[at : at + b, :])
            start = part * half + to * b
            txt_hi[start : start + b, :] = hi
            txt_lo[start : start + b, :] = lo
    txt = (txt_hi[...], txt_lo[...])
    chunk = img.shape[0] // 2
    totals = [jnp.float32(0)] * 3
    for k in range(2):
        part = split(img[k * chunk : (k + 1) * chunk, :])
        sim = dot3(part, txt, ((1,), (1,)))
        logit = temp * sim + shift
        rows = lax.broadcasted_iota(jnp.int32, sim.shape, 0) + (k * chunk - first[0])
        cols = lax.broadcasted_iota(jnp.int32, sim.shape, 1)
        same = (rows == cols) & (cols < b)
        x = jnp.where(same, -logit, logit)
        e = jnp.exp(-jnp.abs(x))
        sig = jnp.where(x >= 0, 1.0, e) / (1.0 + e)
        pair = jnp.where(same, -sig, sig)
        if not images:
            totals[0] += jnp.sum(jnp.maximum(x, 0.0) + jnp.log1p(e))
            totals[1] += jnp.sum(pair * sim)
            totals[2] += jnp.sum(pair)
        pair = split(pair)
        if images:
            term = temp * dot3(pair, txt, ((1,), (0,)))
            for at in range(0, chunk, 8):
                block, tile = (k * chunk + at) // b, (at % b) // 8 * wide
                for j in range(wide):
                    outs[0][block, tile + j, :, :] = term[at : at + 8, j * 128 : (j + 1) * 128]
        else:
            term = temp * dot3(pair, part, ((0,), (0,)))
            for ref, here in zip(outs, (term[:half], term[half:])):
                ref[...] = here if k == 0 else ref[...] + here
    if not images:
        row = lax.broadcasted_iota(jnp.int32, outs[2].shape, 0)
        outs[2][...] = jnp.where(row == 0, totals[0], jnp.where(row == 1, totals[1], totals[2]))


def tile_terms(images, scal, first, img, own, other, b):
    n, d = img.shape
    half = own.shape[0]
    m = 2 * half
    shapes = [(n // b, b * d // 1024 + 1, 8, 128)] if images else [(half, d), (half, d), (8, 128)]
    smem, vmem = pl.BlockSpec(memory_space=pltpu.SMEM), pl.BlockSpec(memory_space=pltpu.VMEM)
    return pl.pallas_call(
        functools.partial(tile_kernel, b, images),
        out_shape=[jax.ShapeDtypeStruct(shape, jnp.float32) for shape in shapes],
        in_specs=[smem, smem, vmem, vmem, vmem],
        out_specs=[vmem] * len(shapes),
        scratch_shapes=[pltpu.VMEM((m, d), jnp.bfloat16), pltpu.VMEM((m, d), jnp.bfloat16)],
        compiler_params=pltpu.CompilerParams(vmem_limit_bytes=20 * 1024 * 1024),
        cost_estimate=pl.CostEstimate(flops=12 * n * m * d, bytes_accessed=8 * (n + m) * d, transcendentals=3 * n * m),
        name="image_tile" if images else "text_tile",
    )(scal, first, img, own, other)


def spread_sum(v, axes):
    n = lax.axis_size(axes)
    return jnp.sum(lax.all_to_all(jnp.broadcast_to(v[None], (n,) + v.shape), axes, 0, 0, tiled=True), axis=0)


def per_device(images, texts, log_temp, bias):
    b = images.shape[0]
    temp = jnp.exp(log_temp[0])
    shift = bias[0]
    unit_img, norm_img = normalize(images)
    unit_txt, norm_txt = normalize(texts)
    img = gather(unit_img, PLANE)
    own, other = gather_txt(unit_txt)
    first_row = jnp.reshape(lax.axis_index(PLANE) * b, (1,)).astype(jnp.int32)
    operands = (jnp.stack([temp, shift]), first_row, img, own, other)
    grad_own, message, sums = tile_terms(False, *operands, b)
    grad_txt = fold(grad_own + swap_core(message), 1)
    sums = spread_sum(sums, DEPTH + ("core",))
    (tiles,) = tile_terms(True, *operands, b)
    sums, grad_txt = lax.optimization_barrier((sums, grad_txt))
    tiles = jnp.sum(exchange(tiles.at[:, -1].set(sums[None]), PLANE), axis=0)
    wide = img.shape[1] // 128
    grad_unit_img = jnp.swapaxes(tiles[:-1].reshape(b // 8, wide, 8, 128), 1, 2).reshape(b, -1)
    sums = tiles[-1]
    grad_unit_txt = fold(fold(fold(grad_txt, 2), 4), 8)
    loss_all, temp_all, bias_all = (sums[i, 0] for i in range(3))
    total_rows = jnp.float32(b * 1024)
    loss = jnp.reshape(loss_all / total_rows, (1,))
    d_log_temp = jnp.reshape(temp * temp_all / total_rows, (1,))
    d_bias = jnp.reshape(bias_all / total_rows, (1,))
    grad_images = unnormalize(unit_img, norm_img, grad_unit_img)
    grad_texts = unnormalize(unit_txt, norm_txt, grad_unit_txt)
    return (loss, d_log_temp, d_bias, grad_images, grad_texts)


def solution(mesh):
    fine = Mesh(mesh.devices.reshape(SIZES), AXES)
    rows = P(AXES, None)
    return jax.shard_map(
        per_device, mesh=fine, in_specs=(rows, rows, P(), P()), out_specs=(P(), P(), P(), rows, rows), check_vma=False
    )
```

```python
import functools

import jax
import jax.numpy as jnp
from jax import lax
from jax.experimental import pallas as pl
from jax.experimental.pallas import tpu as pltpu
from jax.sharding import Mesh, PartitionSpec as P

AXES = ("y", "z_lo", "x", "z_hi", "core")
SIZES = (8, 8, 4, 2, 2)
PLANE = ("y", "x")
DEPTH = ("z_lo", "z_hi")


def normalize(x):
    norm = jnp.sqrt(jnp.sum(x * x, axis=1, keepdims=True) + 1e-06)
    return (x / norm, norm)


def unnormalize(unit, norm, grad_unit):
    inner = jnp.sum(unit * grad_unit, axis=1, keepdims=True)
    return (grad_unit - unit * inner) / norm


def place(z, core):
    return ((z % 8) * 2 + z // 8) * 2 + core


def recv(v, step):
    pairs = []
    for core in range(2):
        for z in range(16):
            pairs.append((place((z + (step if core == 0 else -step)) % 16, core), place(z, core)))
    return lax.ppermute(v, DEPTH + ("core",), pairs)


def send(v, step):
    return recv(v, -step)


def swap_core(v):
    return lax.ppermute(v, "core", [(0, 1), (1, 0)])


def cat(*parts):
    return jnp.concatenate(parts, axis=0)


BROUGHT = (0, 4, 2, 6, -4, -2, -6, 8, 1, 5, 3, 7, -1, -5, -3, -7)
HALVED = (0, 8, 4, -4, 2, -6, 6, -2, 1, -7, 5, -3, 3, -5, 7, -1)


def gather_txt(txt):
    p4, m4 = recv(txt, 4), recv(txt, -4)
    even_up, even_down = cat(txt, p4), cat(txt, m4)
    p2, m2 = recv(even_up, 2), recv(even_down, -2)
    far = recv(p4, 4)
    p1, m1 = recv(cat(even_up, p2), 1), recv(cat(even_down, m2), -1)
    own = cat(even_up, p2, m4, m2, far, p1, m1)
    return (own, swap_core(own))


def scatter_txt(g, s):
    for step in (0, 1, 2, 4, 8):
        half = g.shape[0] // 2
        message = cat(g[half:], s)
        came = send(message, step) if step else swap_core(message)
        g, s = g[:half] + came[:half], s + came[half:]
    return (g, s)


def exchange(v, axes):
    return lax.all_to_all(v, axes, 0, 0, tiled=True)


def gather(v, axes):
    n = lax.axis_size(axes)
    return exchange(jnp.broadcast_to(v[None], (n,) + v.shape).reshape(n * v.shape[0], -1), axes)


def scatter(g, axes):
    n = lax.axis_size(axes)
    return jnp.sum(exchange(g, axes).reshape(n, g.shape[0] // n, -1), axis=0)


def split(x):
    hi = x.astype(jnp.bfloat16)
    return (hi, (x - hi.astype(jnp.float32)).astype(jnp.bfloat16))


def dot3(a, b, dims):
    def dot(x, y):
        return lax.dot_general(x, y, (dims, ((), ())), preferred_element_type=jnp.float32)

    return dot(a[0], b[0]) + (dot(a[0], b[1]) + dot(a[1], b[0]))


def tile_kernel(b, scal, first, img, own, other, grad_img, grad_txt, sums, txt_hi, txt_lo):
    temp, shift = scal[0], scal[1]
    half = own.shape[0]
    for part, ref in enumerate((own, other)):
        for to, z in enumerate(HALVED):
            at = BROUGHT.index(z) * b
            hi, lo = split(ref[at : at + b, :])
            start = part * half + to * b
            txt_hi[start : start + b, :] = hi
            txt_lo[start : start + b, :] = lo
    txt = (txt_hi[...], txt_lo[...])
    chunk = img.shape[0] // 2
    totals = [jnp.float32(0)] * 3
    for k in range(2):
        part = split(img[k * chunk : (k + 1) * chunk, :])
        sim = dot3(part, txt, ((1,), (1,)))
        logit = temp * sim + shift
        rows = lax.broadcasted_iota(jnp.int32, sim.shape, 0) + (k * chunk - first[0])
        cols = lax.broadcasted_iota(jnp.int32, sim.shape, 1)
        same = (rows == cols) & (cols < b)
        x = jnp.where(same, -logit, logit)
        e = jnp.exp(-jnp.abs(x))
        sig = jnp.where(x >= 0, 1.0, e) / (1.0 + e)
        pair = jnp.where(same, -sig, sig)
        totals[0] += jnp.sum(jnp.maximum(x, 0.0) + jnp.log1p(e))
        totals[1] += jnp.sum(pair * sim)
        totals[2] += jnp.sum(pair)
        pair = split(pair)
        grad_img[k * chunk : (k + 1) * chunk, :] = temp * dot3(pair, txt, ((1,), (0,)))
        term = temp * dot3(pair, part, ((0,), (0,)))
        grad_txt[...] = term if k == 0 else grad_txt[...] + term
    row = lax.broadcasted_iota(jnp.int32, sums.shape, 0)
    sums[...] = jnp.where(row == 0, totals[0], jnp.where(row == 1, totals[1], totals[2]))


def tile_terms(scal, first, img, own, other, b):
    n, d = img.shape
    m = 2 * own.shape[0]
    smem, vmem = pl.BlockSpec(memory_space=pltpu.SMEM), pl.BlockSpec(memory_space=pltpu.VMEM)
    return pl.pallas_call(
        functools.partial(tile_kernel, b),
        out_shape=(
            jax.ShapeDtypeStruct((n, d), jnp.float32),
            jax.ShapeDtypeStruct((m, d), jnp.float32),
            jax.ShapeDtypeStruct((8, 128), jnp.float32),
        ),
        in_specs=[smem, smem, vmem, vmem, vmem],
        out_specs=(vmem, vmem, vmem),
        scratch_shapes=[pltpu.VMEM((m, d), jnp.bfloat16), pltpu.VMEM((m, d), jnp.bfloat16)],
        compiler_params=pltpu.CompilerParams(vmem_limit_bytes=40 * 1024 * 1024),
        cost_estimate=pl.CostEstimate(flops=18 * n * m * d, bytes_accessed=8 * (n + m) * d, transcendentals=3 * n * m),
        name="pair_tile",
    )(scal, first, img, own, other)


def spread_sum(v, axes):
    n = lax.axis_size(axes)
    return jnp.sum(lax.all_to_all(jnp.broadcast_to(v[None], (n,) + v.shape), axes, 0, 0, tiled=True), axis=0)


def per_device(images, texts, log_temp, bias):
    b = images.shape[0]
    temp = jnp.exp(log_temp[0])
    shift = bias[0]
    unit_img, norm_img = normalize(images)
    unit_txt, norm_txt = normalize(texts)
    img = gather(unit_img, PLANE)
    own, other = gather_txt(unit_txt)
    first_row = jnp.reshape(lax.axis_index(PLANE) * b, (1,)).astype(jnp.int32)
    grad_img, grad_txt, sums = tile_terms(jnp.stack([temp, shift]), first_row, img, own, other, b)
    sums = jnp.pad(sums, ((0, 0), (0, img.shape[1] - 128)))
    grad_unit_img = scatter(grad_img, PLANE)
    grad_unit_txt, sums = scatter_txt(grad_txt, sums)
    sums, grad_unit_img = lax.optimization_barrier((sums, grad_unit_img))
    sums = spread_sum(sums[:, :128], PLANE)
    loss_all, temp_all, bias_all = (sums[i, 0] for i in range(3))
    total_rows = jnp.float32(b * 1024)
    loss = jnp.reshape(loss_all / total_rows, (1,))
    d_log_temp = jnp.reshape(temp * temp_all / total_rows, (1,))
    d_bias = jnp.reshape(bias_all / total_rows, (1,))
    grad_images = unnormalize(unit_img, norm_img, grad_unit_img)
    grad_texts = unnormalize(unit_txt, norm_txt, grad_unit_txt)
    return (loss, d_log_temp, d_bias, grad_images, grad_texts)


def solution(mesh):
    fine = Mesh(mesh.devices.reshape(SIZES), AXES)
    rows = P(AXES, None)
    return jax.shard_map(
        per_device, mesh=fine, in_specs=(rows, rows, P(), P()), out_specs=(P(), P(), P(), rows, rows), check_vma=False
    )
```

```python
import functools

import jax
import jax.numpy as jnp
from jax import lax
from jax.experimental import pallas as pl
from jax.experimental.pallas import tpu as pltpu
from jax.sharding import Mesh, PartitionSpec as P

AXES = ("y", "z_lo", "x", "z_hi", "core")
SIZES = (8, 8, 4, 2, 2)
PLANE = ("y", "x")
DEPTH = ("z_lo", "z_hi")


def normalize(x):
    norm = jnp.sqrt(jnp.sum(x * x, axis=1, keepdims=True) + 1e-06)
    return (x / norm, norm)


def unnormalize(unit, norm, grad_unit):
    inner = jnp.sum(unit * grad_unit, axis=1, keepdims=True)
    return (grad_unit - unit * inner) / norm


def place(z, core):
    return ((z % 8) * 2 + z // 8) * 2 + core


def recv(v, step):
    pairs = []
    for core in range(2):
        for z in range(16):
            pairs.append((place((z + (step if core == 0 else -step)) % 16, core), place(z, core)))
    return lax.ppermute(v, DEPTH + ("core",), pairs)


def send(v, step):
    return recv(v, -step)


def swap_core(v):
    return lax.ppermute(v, "core", [(0, 1), (1, 0)])


def cat(*parts):
    return jnp.concatenate(parts, axis=0)


BROUGHT = (0, 4, 2, 6, -4, -2, -6, 8, 1, 5, 3, 7, -1, -5, -3, -7)
HALVED = (0, 8, 4, -4, 2, -6, 6, -2, 1, -7, 5, -3, 3, -5, 7, -1)


def gather_txt(txt):
    p4, m4 = recv(txt, 4), recv(txt, -4)
    even_up, even_down = cat(txt, p4), cat(txt, m4)
    p2, m2 = recv(even_up, 2), recv(even_down, -2)
    far = recv(p4, 4)
    p1, m1 = recv(cat(even_up, p2), 1), recv(cat(even_down, m2), -1)
    own = cat(even_up, p2, m4, m2, far, p1, m1)
    return (own, swap_core(own))


def scatter_txt(g, message):
    s = message[-8:]
    came = swap_core(message)
    for step in (1, 2, 4, 8):
        g, s = g + came[:-8], s + came[-8:]
        half = g.shape[0] // 2
        came = send(cat(g[half:], s), step)
        g = g[:half]
    return (g + came[:-8], s + came[-8:])


def exchange(v, axes):
    return lax.all_to_all(v, axes, 0, 0, tiled=True)


def gather(v, axes):
    n = lax.axis_size(axes)
    return exchange(jnp.broadcast_to(v[None], (n,) + v.shape).reshape(n * v.shape[0], -1), axes)


def scatter(g, axes):
    n = lax.axis_size(axes)
    return jnp.sum(exchange(g, axes).reshape(n, g.shape[0] // n, -1), axis=0)


def split(x):
    hi = x.astype(jnp.bfloat16)
    return (hi, (x - hi.astype(jnp.float32)).astype(jnp.bfloat16))


def dot3(a, b, dims):
    def dot(x, y):
        return lax.dot_general(x, y, (dims, ((), ())), preferred_element_type=jnp.float32)

    return dot(a[0], b[0]) + (dot(a[0], b[1]) + dot(a[1], b[0]))


def tile_kernel(b, scal, first, img, own, other, grad_img, grad_own, message, txt_hi, txt_lo):
    temp, shift = scal[0], scal[1]
    half = own.shape[0]
    for part, ref in enumerate((own, other)):
        for to, z in enumerate(HALVED):
            at = BROUGHT.index(z) * b
            hi, lo = split(ref[at : at + b, :])
            start = part * half + to * b
            txt_hi[start : start + b, :] = hi
            txt_lo[start : start + b, :] = lo
    txt = (txt_hi[...], txt_lo[...])
    chunk = img.shape[0] // 2
    totals = [jnp.float32(0)] * 3
    for k in range(2):
        part = split(img[k * chunk : (k + 1) * chunk, :])
        sim = dot3(part, txt, ((1,), (1,)))
        logit = temp * sim + shift
        rows = lax.broadcasted_iota(jnp.int32, sim.shape, 0) + (k * chunk - first[0])
        cols = lax.broadcasted_iota(jnp.int32, sim.shape, 1)
        same = (rows == cols) & (cols < b)
        x = jnp.where(same, -logit, logit)
        e = jnp.exp(-jnp.abs(x))
        sig = jnp.where(x >= 0, 1.0, e) / (1.0 + e)
        pair = jnp.where(same, -sig, sig)
        totals[0] += jnp.sum(jnp.maximum(x, 0.0) + jnp.log1p(e))
        totals[1] += jnp.sum(pair * sim)
        totals[2] += jnp.sum(pair)
        pair = split(pair)
        grad_img[k * chunk : (k + 1) * chunk, :] = temp * dot3(pair, txt, ((1,), (0,)))
        term = temp * dot3(pair, part, ((0,), (0,)))
        grad_own[...] = term[:half] if k == 0 else grad_own[...] + term[:half]
        message[:half, :] = term[half:] if k == 0 else message[:half, :] + term[half:]
    row = lax.broadcasted_iota(jnp.int32, (8, img.shape[1]), 0)
    message[half:, :] = jnp.where(row == 0, totals[0], jnp.where(row == 1, totals[1], totals[2]))


def tile_terms(scal, first, img, own, other, b):
    n, d = img.shape
    half = own.shape[0]
    m = 2 * half
    smem, vmem = pl.BlockSpec(memory_space=pltpu.SMEM), pl.BlockSpec(memory_space=pltpu.VMEM)
    return pl.pallas_call(
        functools.partial(tile_kernel, b),
        out_shape=(
            jax.ShapeDtypeStruct((n, d), jnp.float32),
            jax.ShapeDtypeStruct((half, d), jnp.float32),
            jax.ShapeDtypeStruct((half + 8, d), jnp.float32),
        ),
        in_specs=[smem, smem, vmem, vmem, vmem],
        out_specs=(vmem, vmem, vmem),
        scratch_shapes=[pltpu.VMEM((m, d), jnp.bfloat16), pltpu.VMEM((m, d), jnp.bfloat16)],
        compiler_params=pltpu.CompilerParams(vmem_limit_bytes=40 * 1024 * 1024),
        cost_estimate=pl.CostEstimate(flops=18 * n * m * d, bytes_accessed=8 * (n + m) * d, transcendentals=3 * n * m),
        name="pair_tile",
    )(scal, first, img, own, other)


def spread_sum(v, axes):
    n = lax.axis_size(axes)
    return jnp.sum(lax.all_to_all(jnp.broadcast_to(v[None], (n,) + v.shape), axes, 0, 0, tiled=True), axis=0)


def per_device(images, texts, log_temp, bias):
    b = images.shape[0]
    temp = jnp.exp(log_temp[0])
    shift = bias[0]
    unit_img, norm_img = normalize(images)
    unit_txt, norm_txt = normalize(texts)
    img = gather(unit_img, PLANE)
    own, other = gather_txt(unit_txt)
    first_row = jnp.reshape(lax.axis_index(PLANE) * b, (1,)).astype(jnp.int32)
    grad_img, grad_own, message = tile_terms(jnp.stack([temp, shift]), first_row, img, own, other, b)
    grad_unit_img = scatter(grad_img, PLANE)
    grad_unit_txt, sums = scatter_txt(grad_own, message)
    sums, grad_unit_img = lax.optimization_barrier((sums, grad_unit_img))
    sums = spread_sum(sums[:, :128], PLANE)
    loss_all, temp_all, bias_all = (sums[i, 0] for i in range(3))
    total_rows = jnp.float32(b * 1024)
    loss = jnp.reshape(loss_all / total_rows, (1,))
    d_log_temp = jnp.reshape(temp * temp_all / total_rows, (1,))
    d_bias = jnp.reshape(bias_all / total_rows, (1,))
    grad_images = unnormalize(unit_img, norm_img, grad_unit_img)
    grad_texts = unnormalize(unit_txt, norm_txt, grad_unit_txt)
    return (loss, d_log_temp, d_bias, grad_images, grad_texts)


def solution(mesh):
    fine = Mesh(mesh.devices.reshape(SIZES), AXES)
    rows = P(AXES, None)
    return jax.shard_map(
        per_device, mesh=fine, in_specs=(rows, rows, P(), P()), out_specs=(P(), P(), P(), rows, rows), check_vma=False
    )
```

```python
import functools

import jax
import jax.numpy as jnp
from jax import lax
from jax.experimental import pallas as pl
from jax.experimental.pallas import tpu as pltpu
from jax.sharding import Mesh, PartitionSpec as P

AXES = ("y", "z_lo", "x", "z_hi", "core")
SIZES = (8, 8, 4, 2, 2)
PLANE = ("y", "x")
DEPTH = ("z_lo", "z_hi")


def normalize(x):
    norm = jnp.sqrt(jnp.sum(x * x, axis=1, keepdims=True) + 1e-06)
    return (x / norm, norm)


def unnormalize(unit, norm, grad_unit):
    inner = jnp.sum(unit * grad_unit, axis=1, keepdims=True)
    return (grad_unit - unit * inner) / norm


def place(z, core):
    return ((z % 8) * 2 + z // 8) * 2 + core


def recv(v, step):
    pairs = []
    for core in range(2):
        for z in range(16):
            pairs.append((place((z + (step if core == 0 else -step)) % 16, core), place(z, core)))
    return lax.ppermute(v, DEPTH + ("core",), pairs)


def send(v, step):
    return recv(v, -step)


def swap_core(v):
    return lax.ppermute(v, "core", [(0, 1), (1, 0)])


def cat(*parts):
    return jnp.concatenate(parts, axis=0)


BROUGHT = (0, 4, 2, 6, -4, -2, -6, 8, 1, 5, 3, 7, -1, -5, -3, -7)
HALVED = (0, 8, 4, -4, 2, -6, 6, -2, 1, -7, 5, -3, 3, -5, 7, -1)


def gather_txt(txt):
    p4, m4 = recv(txt, 4), recv(txt, -4)
    even_up, even_down = cat(txt, p4), cat(txt, m4)
    p2, m2 = recv(even_up, 2), recv(even_down, -2)
    far = recv(p4, 4)
    p1, m1 = recv(cat(even_up, p2), 1), recv(cat(even_down, m2), -1)
    own = cat(even_up, p2, m4, m2, far, p1, m1)
    return (own, swap_core(own))


def scatter_txt(g, message):
    s = message[-1:]
    came = swap_core(message)
    for step in (1, 2, 4, 8):
        g, s = g + came[:-1], s + came[-1:]
        half = g.shape[0] // 2
        came = send(cat(g[half:], s), step)
        g = g[:half]
    return (g + came[:-1], s + came[-1:])


def exchange(v, axes):
    return lax.all_to_all(v, axes, 0, 0, tiled=True)


def gather(v, axes):
    n = lax.axis_size(axes)
    return exchange(jnp.broadcast_to(v[None], (n,) + v.shape).reshape(n * v.shape[0], -1), axes)


def scatter(g, axes):
    n = lax.axis_size(axes)
    return jnp.sum(exchange(g, axes).reshape(n, g.shape[0] // n, -1), axis=0)


def split(x):
    hi = x.astype(jnp.bfloat16)
    return (hi, (x - hi.astype(jnp.float32)).astype(jnp.bfloat16))


def dot3(a, b, dims):
    def dot(x, y):
        return lax.dot_general(x, y, (dims, ((), ())), preferred_element_type=jnp.float32)

    return dot(a[0], b[0]) + (dot(a[0], b[1]) + dot(a[1], b[0]))


def tile_kernel(b, scal, first, img, own, other, grad_img, grad_own, message, txt_hi, txt_lo):
    temp, shift = scal[0], scal[1]
    half = own.shape[0]
    wide = img.shape[1] // 128
    for part, ref in enumerate((own, other)):
        for to, z in enumerate(HALVED):
            at = BROUGHT.index(z) * b
            hi, lo = split(ref[at : at + b, :])
            start = part * half + to * b
            txt_hi[start : start + b, :] = hi
            txt_lo[start : start + b, :] = lo
    txt = (txt_hi[...], txt_lo[...])
    chunk = img.shape[0] // 2
    totals = [jnp.float32(0)] * 3
    for k in range(2):
        part = split(img[k * chunk : (k + 1) * chunk, :])
        sim = dot3(part, txt, ((1,), (1,)))
        logit = temp * sim + shift
        rows = lax.broadcasted_iota(jnp.int32, sim.shape, 0) + (k * chunk - first[0])
        cols = lax.broadcasted_iota(jnp.int32, sim.shape, 1)
        same = (rows == cols) & (cols < b)
        x = jnp.where(same, -logit, logit)
        e = jnp.exp(-jnp.abs(x))
        sig = jnp.where(x >= 0, 1.0, e) / (1.0 + e)
        pair = jnp.where(same, -sig, sig)
        totals[0] += jnp.sum(jnp.maximum(x, 0.0) + jnp.log1p(e))
        totals[1] += jnp.sum(pair * sim)
        totals[2] += jnp.sum(pair)
        pair = split(pair)
        grad_img[k * chunk : (k + 1) * chunk, :] = temp * dot3(pair, txt, ((1,), (0,)))
        term = temp * dot3(pair, part, ((0,), (0,)))
        for at in range(0, 2 * half, 8):
            ref, tile = (grad_own, at // 8 * wide) if at < half else (message, (at - half) // 8 * wide)
            for j in range(wide):
                value = term[at : at + 8, j * 128 : (j + 1) * 128]
                ref[tile + j, :, :] = value if k == 0 else ref[tile + j, :, :] + value
    row = lax.broadcasted_iota(jnp.int32, (8, 128), 0)
    message[half // 8 * wide, :, :] = jnp.where(row == 0, totals[0], jnp.where(row == 1, totals[1], totals[2]))


def tile_terms(scal, first, img, own, other, b):
    n, d = img.shape
    half = own.shape[0]
    m = 2 * half
    smem, vmem = pl.BlockSpec(memory_space=pltpu.SMEM), pl.BlockSpec(memory_space=pltpu.VMEM)
    return pl.pallas_call(
        functools.partial(tile_kernel, b),
        out_shape=(
            jax.ShapeDtypeStruct((n, d), jnp.float32),
            jax.ShapeDtypeStruct((half * d // 1024, 8, 128), jnp.float32),
            jax.ShapeDtypeStruct((half * d // 1024 + 1, 8, 128), jnp.float32),
        ),
        in_specs=[smem, smem, vmem, vmem, vmem],
        out_specs=(vmem, vmem, vmem),
        scratch_shapes=[pltpu.VMEM((m, d), jnp.bfloat16), pltpu.VMEM((m, d), jnp.bfloat16)],
        compiler_params=pltpu.CompilerParams(vmem_limit_bytes=40 * 1024 * 1024),
        cost_estimate=pl.CostEstimate(flops=18 * n * m * d, bytes_accessed=8 * (n + m) * d, transcendentals=3 * n * m),
        name="pair_tile",
    )(scal, first, img, own, other)


def spread_sum(v, axes):
    n = lax.axis_size(axes)
    return jnp.sum(lax.all_to_all(jnp.broadcast_to(v[None], (n,) + v.shape), axes, 0, 0, tiled=True), axis=0)


def per_device(images, texts, log_temp, bias):
    b = images.shape[0]
    temp = jnp.exp(log_temp[0])
    shift = bias[0]
    unit_img, norm_img = normalize(images)
    unit_txt, norm_txt = normalize(texts)
    img = gather(unit_img, PLANE)
    own, other = gather_txt(unit_txt)
    first_row = jnp.reshape(lax.axis_index(PLANE) * b, (1,)).astype(jnp.int32)
    grad_img, grad_own, message = tile_terms(jnp.stack([temp, shift]), first_row, img, own, other, b)
    grad_unit_img = scatter(grad_img, PLANE)
    tiles, sums = scatter_txt(grad_own, message)
    grad_unit_txt = jnp.swapaxes(tiles.reshape(b // 8, -1, 8, 128), 1, 2).reshape(b, -1)
    sums, grad_unit_img = lax.optimization_barrier((sums, grad_unit_img))
    sums = spread_sum(sums[0], PLANE)
    loss_all, temp_all, bias_all = (sums[i, 0] for i in range(3))
    total_rows = jnp.float32(b * 1024)
    loss = jnp.reshape(loss_all / total_rows, (1,))
    d_log_temp = jnp.reshape(temp * temp_all / total_rows, (1,))
    d_bias = jnp.reshape(bias_all / total_rows, (1,))
    grad_images = unnormalize(unit_img, norm_img, grad_unit_img)
    grad_texts = unnormalize(unit_txt, norm_txt, grad_unit_txt)
    return (loss, d_log_temp, d_bias, grad_images, grad_texts)


def solution(mesh):
    fine = Mesh(mesh.devices.reshape(SIZES), AXES)
    rows = P(AXES, None)
    return jax.shard_map(
        per_device, mesh=fine, in_specs=(rows, rows, P(), P()), out_specs=(P(), P(), P(), rows, rows), check_vma=False
    )
```

```python
import functools

import jax
import jax.numpy as jnp
from jax import lax
from jax.experimental import pallas as pl
from jax.experimental.pallas import tpu as pltpu
from jax.sharding import Mesh, PartitionSpec as P

AXES = ("y", "z_lo", "x", "z_hi", "core")
SIZES = (8, 8, 4, 2, 2)
PLANE = ("y", "x")
DEPTH = ("z_lo", "z_hi")


def normalize(x):
    norm = jnp.sqrt(jnp.sum(x * x, axis=1, keepdims=True) + 1e-06)
    return (x / norm, norm)


def unnormalize(unit, norm, grad_unit):
    inner = jnp.sum(unit * grad_unit, axis=1, keepdims=True)
    return (grad_unit - unit * inner) / norm


def place(z, core):
    return ((z % 8) * 2 + z // 8) * 2 + core


def recv(v, step):
    pairs = []
    for core in range(2):
        for z in range(16):
            pairs.append((place((z + (step if core == 1 else -step)) % 16, core), place(z, core)))
    return lax.ppermute(v, DEPTH + ("core",), pairs)


def send(v, step):
    return recv(v, -step)


def swap_core(v):
    return lax.ppermute(v, "core", [(0, 1), (1, 0)])


def cat(*parts):
    return jnp.concatenate(parts, axis=0)


BROUGHT = (0, 4, 2, 6, -4, -2, -6, 8, 1, 5, 3, 7, -1, -5, -3, -7)
HALVED = (0, 8, -4, 4, -2, 6, -6, 2, -1, 7, -5, 3, -3, 5, -7, 1)


def gather_txt(txt):
    p4, m4 = recv(txt, 4), recv(txt, -4)
    even_up, even_down = cat(txt, p4), cat(txt, m4)
    p2, m2 = recv(even_up, 2), recv(even_down, -2)
    far = recv(p4, 4)
    p1, m1 = recv(cat(even_up, p2), 1), recv(cat(even_down, m2), -1)
    own = cat(even_up, p2, m4, m2, far, p1, m1)
    return (own, swap_core(own))


def scatter_txt(g, message):
    g = g + swap_core(message)
    for step in (-1, -2, -4, -8):
        half = g.shape[0] // 2
        came = send(g[half:], step)
        last = lax.broadcasted_iota(jnp.int32, came.shape, 0) == half
        g = jnp.where(last, g[-1:], g[: half + 1]) + came
    return (g[:-1], g[-1])


def exchange(v, axes):
    return lax.all_to_all(v, axes, 0, 0, tiled=True)


def gather(v, axes):
    n = lax.axis_size(axes)
    return exchange(jnp.broadcast_to(v[None], (n,) + v.shape).reshape(n * v.shape[0], -1), axes)


def scatter(g, axes):
    n = lax.axis_size(axes)
    return jnp.sum(exchange(g, axes).reshape(n, g.shape[0] // n, -1), axis=0)


def split(x):
    hi = x.astype(jnp.bfloat16)
    return (hi, (x - hi.astype(jnp.float32)).astype(jnp.bfloat16))


def dot3(a, b, dims):
    def dot(x, y):
        return lax.dot_general(x, y, (dims, ((), ())), preferred_element_type=jnp.float32)

    return dot(a[0], b[0]) + (dot(a[0], b[1]) + dot(a[1], b[0]))


def tile_kernel(b, scal, first, img, own, other, grad_img, grad_own, message, txt_hi, txt_lo):
    temp, shift = scal[0], scal[1]
    half = own.shape[0]
    wide = img.shape[1] // 128
    for part, ref in enumerate((own, other)):
        for to, z in enumerate(HALVED):
            at = BROUGHT.index(z) * b
            hi, lo = split(ref[at : at + b, :])
            start = part * half + to * b
            txt_hi[start : start + b, :] = hi
            txt_lo[start : start + b, :] = lo
    txt = (txt_hi[...], txt_lo[...])
    chunk = img.shape[0] // 2
    totals = [jnp.float32(0)] * 3
    for k in range(2):
        part = split(img[k * chunk : (k + 1) * chunk, :])
        sim = dot3(part, txt, ((1,), (1,)))
        logit = temp * sim + shift
        rows = lax.broadcasted_iota(jnp.int32, sim.shape, 0) + (k * chunk - first[0])
        cols = lax.broadcasted_iota(jnp.int32, sim.shape, 1)
        same = (rows == cols) & (cols < b)
        x = jnp.where(same, -logit, logit)
        e = jnp.exp(-jnp.abs(x))
        sig = jnp.where(x >= 0, 1.0, e) / (1.0 + e)
        pair = jnp.where(same, -sig, sig)
        totals[0] += jnp.sum(jnp.maximum(x, 0.0) + jnp.log1p(e))
        totals[1] += jnp.sum(pair * sim)
        totals[2] += jnp.sum(pair)
        pair = split(pair)
        grad_img[k * chunk : (k + 1) * chunk, :] = temp * dot3(pair, txt, ((1,), (0,)))
        term = temp * dot3(pair, part, ((0,), (0,)))
        for at in range(0, 2 * half, 8):
            ref, tile = (grad_own, at // 8 * wide) if at < half else (message, (at - half) // 8 * wide)
            for j in range(wide):
                value = term[at : at + 8, j * 128 : (j + 1) * 128]
                ref[tile + j, :, :] = value if k == 0 else ref[tile + j, :, :] + value
    row = lax.broadcasted_iota(jnp.int32, (8, 128), 0)
    grad_own[half // 8 * wide, :, :] = message[half // 8 * wide, :, :] = jnp.where(row == 0, totals[0], jnp.where(row == 1, totals[1], totals[2]))


def tile_terms(scal, first, img, own, other, b):
    n, d = img.shape
    half = own.shape[0]
    m = 2 * half
    smem, vmem = pl.BlockSpec(memory_space=pltpu.SMEM), pl.BlockSpec(memory_space=pltpu.VMEM)
    return pl.pallas_call(
        functools.partial(tile_kernel, b),
        out_shape=(
            jax.ShapeDtypeStruct((n, d), jnp.float32),
            jax.ShapeDtypeStruct((half * d // 1024 + 1, 8, 128), jnp.float32),
            jax.ShapeDtypeStruct((half * d // 1024 + 1, 8, 128), jnp.float32),
        ),
        in_specs=[smem, smem, vmem, vmem, vmem],
        out_specs=(vmem, vmem, vmem),
        scratch_shapes=[pltpu.VMEM((m, d), jnp.bfloat16), pltpu.VMEM((m, d), jnp.bfloat16)],
        compiler_params=pltpu.CompilerParams(vmem_limit_bytes=40 * 1024 * 1024),
        cost_estimate=pl.CostEstimate(flops=18 * n * m * d, bytes_accessed=8 * (n + m) * d, transcendentals=3 * n * m),
        name="pair_tile",
    )(scal, first, img, own, other)


def spread_sum(v, axes):
    n = lax.axis_size(axes)
    return jnp.sum(lax.all_to_all(jnp.broadcast_to(v[None], (n,) + v.shape), axes, 0, 0, tiled=True), axis=0)


def per_device(images, texts, log_temp, bias):
    b = images.shape[0]
    temp = jnp.exp(log_temp[0])
    shift = bias[0]
    unit_img, norm_img = normalize(images)
    unit_txt, norm_txt = normalize(texts)
    img = gather(unit_img, PLANE)
    own, other = gather_txt(unit_txt)
    first_row = jnp.reshape(lax.axis_index(PLANE) * b, (1,)).astype(jnp.int32)
    grad_img, grad_own, message = tile_terms(jnp.stack([temp, shift]), first_row, img, own, other, b)
    grad_unit_img = scatter(grad_img, PLANE)
    tiles, sums = scatter_txt(grad_own, message)
    grad_unit_txt = jnp.swapaxes(tiles.reshape(b // 8, -1, 8, 128), 1, 2).reshape(b, -1)
    sums, grad_unit_img = lax.optimization_barrier((sums, grad_unit_img))
    sums = spread_sum(sums, PLANE)
    loss_all, temp_all, bias_all = (sums[i, 0] for i in range(3))
    total_rows = jnp.float32(b * 1024)
    loss = jnp.reshape(loss_all / total_rows, (1,))
    d_log_temp = jnp.reshape(temp * temp_all / total_rows, (1,))
    d_bias = jnp.reshape(bias_all / total_rows, (1,))
    grad_images = unnormalize(unit_img, norm_img, grad_unit_img)
    grad_texts = unnormalize(unit_txt, norm_txt, grad_unit_txt)
    return (loss, d_log_temp, d_bias, grad_images, grad_texts)


def solution(mesh):
    fine = Mesh(mesh.devices.reshape(SIZES), AXES)
    rows = P(AXES, None)
    return jax.shard_map(
        per_device, mesh=fine, in_specs=(rows, rows, P(), P()), out_specs=(P(), P(), P(), rows, rows), check_vma=False
    )
```
